256 devices in a mesh: wide: 128 (over y, z, x_lo, core), row: 2 (over x_hi).
Axes of the slice: x: 4 (x_hi: 2, x_lo: 2; x = x_hi * 2 + x_lo), y: 4, z: 8, core: 2. Of those that a mesh axis runs over, the one named last changes fastest.
Arguments:
- pair: bfloat16 [512, 512, 128], P('wide', 'row'), may hold values from -6 to 6
- token_valid: int32 [512], replicated, may hold values 0 or 1
- w_pair: bfloat16 [128, 512], replicated, may hold values from -0.5 to 0.5
- w_gate: bfloat16 [128, 128], replicated, may hold values from -0.5 to 0.5
- w_out: bfloat16 [128, 128], replicated, may hold values from -0.5 to 0.5
Outputs:
- update: bfloat16 [512, 512, 128], P('wide', 'row')
The draws below stay inside these ranges and needn't reach their ends.
All inputs are finite; a program needn't handle non-finite values.
Results may differ from the reference program's by a relative error of at most 0.017.
Values may be sent and summed in bfloat16 or wider, within the bound.
No kernel may reach another device: no remote copies, remote signals or barrier semaphores. Data moves between devices by JAX's collectives and lax.ppermute only.
A program may use at most 64 MiB of HBM per device.

```python
import jax
import jax.numpy as jnp
from jax import lax

C = 128
HIDDEN_SIZE = 128
ROWS_DEV = 4
N = 512


def plant(drawn, key, low, high):
    place = [jax.random.randint(jax.random.fold_in(key, axis), (), 0, length) for axis, length in enumerate(drawn.shape)]
    main_axis = drawn.shape.index(max(drawn.shape))
    beside = place[:main_axis] + [(place[main_axis] + 1) % drawn.shape[main_axis]] + place[main_axis + 1:]
    return drawn.at[tuple(place)].set(low).at[tuple(beside)].set(high)


def levels(rng, extent, split, least, largest):
    def one(axis_at, parts):
        steps = jax.random.uniform(jax.random.fold_in(jax.random.fold_in(rng, 6), axis_at), (parts,), jnp.float32, least / len(split), largest / len(split))
        return jnp.repeat(jnp.exp(steps), extent[axis_at] // parts).reshape((-1,) + (1,) * (len(extent) - axis_at - 1))

    loudness = one(*split[0])
    for cut in split[1:]:
        loudness = loudness * one(*cut)
    return loudness


def scatter_about(stream_key, shape, width, reach, cuts=(), kind=jnp.bfloat16):
    level = levels(stream_key, shape, cuts, -0.22, 0.18) if cuts else 1.0
    values = jax.random.normal(stream_key, shape, jnp.float32) * width * level
    return jnp.minimum(jnp.maximum(values, -reach), reach).astype(kind)


def setup_inputs(seed: int = 0) -> dict:
    streams_of = jax.random.split(jax.random.key(seed), 6)
    return {
        "pair": scatter_about(streams_of[0], (N, N, C), 1.0, 6.0, ((0, 128), (1, 2))),
        "token_valid": plant((jax.random.randint(streams_of[1], (N,), 0, 8) < 7).astype(jnp.int32), jax.random.fold_in(streams_of[1], 1), 0, 1),
        "w_pair": scatter_about(streams_of[2], (C, 4 * HIDDEN_SIZE), C ** -0.5, 0.5),
        "w_gate": scatter_about(streams_of[3], (C, C), C ** -0.5, 0.5),
        "w_out": scatter_about(streams_of[4], (HIDDEN_SIZE, C), HIDDEN_SIZE ** -0.5, 0.5),
    }


def normalize(values, axis):
    mean = lax.optimization_barrier(jnp.mean(values, axis=axis, keepdims=True))
    centered = values - mean
    spread = lax.optimization_barrier(jnp.mean(centered * centered, axis=axis, keepdims=True))
    return centered * lax.rsqrt(spread + 1e-05)

def reference(pair, token_valid, w_pair, w_gate, w_out):
    valid = token_valid.astype(jnp.float32)
    blocks = N // ROWS_DEV

    def normed_rows(index):
        rows = lax.dynamic_slice_in_dim(pair, (index * ROWS_DEV).astype(jnp.int32), ROWS_DEV, 0)
        return normalize(rows.astype(jnp.float32), 2).astype(jnp.bfloat16)

    def project(index):
        normed = normed_rows(index)
        proj = jnp.dot(normed.reshape(-1, C), w_pair, preferred_element_type=jnp.float32)
        proj = proj.reshape(ROWS_DEV, N, 4 * HIDDEN_SIZE)
        row_valid = lax.dynamic_slice_in_dim(valid, (index * ROWS_DEV).astype(jnp.int32), ROWS_DEV, 0)
        weight_mask = (row_valid[:, None] * valid[None, :])[:, :, None]
        left = jax.nn.sigmoid(proj[..., :HIDDEN_SIZE]) * proj[..., HIDDEN_SIZE:2 * HIDDEN_SIZE] * weight_mask
        right = jax.nn.sigmoid(proj[..., 2 * HIDDEN_SIZE:3 * HIDDEN_SIZE]) * proj[..., 3 * HIDDEN_SIZE:] * weight_mask
        return (jnp.transpose(left.astype(jnp.bfloat16), (2, 0, 1)), jnp.transpose(right.astype(jnp.bfloat16), (2, 0, 1)))
    left_blocks, right_blocks = lax.map(project, jnp.arange(blocks, dtype=jnp.int32))
    left_all = jnp.transpose(left_blocks, (1, 0, 2, 3)).reshape(HIDDEN_SIZE, N, N)
    right_all = jnp.transpose(right_blocks, (1, 0, 2, 3)).reshape(HIDDEN_SIZE, N, N)

    def plane(pieces):
        return jnp.dot(pieces[0], pieces[1].T, preferred_element_type=jnp.float32).astype(jnp.bfloat16)
    planes = lax.map(plane, (left_all, right_all))

    def finish(index):
        normed = normed_rows(index)
        gating = jax.nn.sigmoid(jnp.dot(normed.reshape(-1, C), w_gate, preferred_element_type=jnp.float32))
        block = lax.dynamic_slice_in_dim(planes, (index * ROWS_DEV).astype(jnp.int32), ROWS_DEV, 1)
        block_norm = normalize(block.astype(jnp.float32), 0).astype(jnp.bfloat16)
        flat = jnp.transpose(block_norm, (1, 2, 0)).reshape(-1, HIDDEN_SIZE)
        mixed = jnp.dot(flat, w_out, preferred_element_type=jnp.float32)
        return (gating * mixed).astype(jnp.bfloat16).reshape(ROWS_DEV, N, C)
    result = lax.map(finish, jnp.arange(blocks, dtype=jnp.int32))
    return result.reshape(N, N, C)
```

```python
import jax
import jax.numpy as jnp
from jax import lax
from jax.sharding import PartitionSpec as P


def normalize(values, axis):
    mean = jnp.mean(values, axis=axis, keepdims=True)
    centered = values - mean
    spread = jnp.mean(centered * centered, axis=axis, keepdims=True)
    return centered * lax.rsqrt(spread + 1e-05)


def chip_groups(wide, row):
    chips = wide // 2
    return [
        [(chip * 2 + core) * row + half for half in range(row) for chip in range(chips)]
        for core in range(2)
    ]


def exchange(blocks, groups):
    return lax.all_to_all(
        blocks, ("wide", "row"), split_axis=0, concat_axis=0, tiled=True, axis_index_groups=groups
    )


def make(wide, row):
    groups = chip_groups(wide, row)
    chips = wide // 2

    def shards(pair, token_valid, w_pair, w_gate, w_out):
        rows_dev, cols_dev, width = pair.shape
        hidden = w_out.shape[0]
        valid = token_valid.astype(jnp.float32)
        row_valid = lax.dynamic_slice_in_dim(
            valid, lax.axis_index("wide") * rows_dev, rows_dev, 0
        )
        col_valid = lax.dynamic_slice_in_dim(valid, lax.axis_index("row") * cols_dev, cols_dev, 0)
        weight_mask = (row_valid[:, None] * col_valid[None, :]).reshape(1, -1)
        normed = normalize(pair.astype(jnp.float32), 2).astype(jnp.bfloat16)
        normed = normed.reshape(-1, width)
        proj = jnp.einsum("de,nd->en", w_pair, normed, preferred_element_type=jnp.float32)
        left = jax.nn.sigmoid(proj[:hidden]) * proj[hidden : 2 * hidden] * weight_mask
        right = jax.nn.sigmoid(proj[2 * hidden : 3 * hidden]) * proj[3 * hidden :] * weight_mask
        sent = jnp.concatenate(
            [
                left.astype(jnp.bfloat16).reshape(hidden, rows_dev, cols_dev),
                right.astype(jnp.bfloat16).reshape(hidden, rows_dev, cols_dev),
            ],
            axis=1,
        )
        got = exchange(sent, groups).reshape(row, chips, 2, rows_dev, cols_dev)
        own_left = got[:, :, 0].reshape(row, chips * rows_dev, cols_dev)
        own_right = got[:, :, 1].reshape(row, chips * rows_dev, cols_dev)
        other_right = lax.ppermute(own_right, "wide", [(i, i ^ 1) for i in range(wide)])
        core = lax.axis_index("wide") % 2
        pairs = jnp.where(
            core == 0,
            jnp.stack([own_right, other_right]),
            jnp.stack([other_right, own_right]),
        )
        plane = jnp.einsum("rik,qrjk->iqj", own_left, pairs, preferred_element_type=jnp.float32)
        plane = plane.astype(jnp.bfloat16).reshape(chips, rows_dev, 2, row, chips // row, rows_dev)
        plane = plane.transpose(3, 0, 1, 4, 2, 5).reshape(row * chips, rows_dev, cols_dev)
        returned = exchange(plane, groups)
        gating = jax.nn.sigmoid(
            jnp.einsum("nd,de->ne", normed, w_gate, preferred_element_type=jnp.float32)
        )
        tri_norm = normalize(returned.astype(jnp.float32), 0).astype(jnp.bfloat16)
        mixed = jnp.einsum(
            "hn,hc->nc", tri_norm.reshape(hidden, -1), w_out, preferred_element_type=jnp.float32
        )
        return (gating * mixed).astype(jnp.bfloat16).reshape(rows_dev, cols_dev, width)

    return shards


def solution(mesh):
    placed = (P("wide", "row", None), P(), P(), P(), P())
    return jax.shard_map(
        make(mesh.shape["wide"], mesh.shape["row"]),
        mesh=mesh,
        in_specs=placed,
        out_specs=P("wide", "row", None),
        check_vma=False,
    )
```

```python
import jax
import jax.numpy as jnp
from jax import lax
from jax.experimental import pallas as pl
from jax.experimental.pallas import tpu as pltpu
from jax.sharding import PartitionSpec as P


def normalize(values, axis):
    mean = jnp.mean(values, axis=axis, keepdims=True)
    centered = values - mean
    spread = jnp.mean(centered * centered, axis=axis, keepdims=True)
    return centered * lax.rsqrt(spread + 1e-05)


def chip_groups(wide, row):
    chips = wide // 2
    return [
        [(chip * 2 + core) * row + half for half in range(row) for chip in range(chips)]
        for core in range(2)
    ]


def exchange(blocks, groups):
    return lax.all_to_all(
        blocks, ("wide", "row"), split_axis=0, concat_axis=0, tiled=True, axis_index_groups=groups
    )


def dot_rows(left, right):
    return lax.dot_general(
        left, right, (((1,), (1,)), ((), ())), preferred_element_type=jnp.float32
    )


def plane_kernel(core_ref, got_ref, other_ref, out_ref):
    blocks, rows, cols = out_ref.shape
    chips = blocks // 2
    size = chips * rows

    def flat(values):
        return values.astype(jnp.float32).reshape(size, cols).astype(jnp.bfloat16)

    own = jnp.zeros((size, size), jnp.float32)
    other = jnp.zeros((size, size), jnp.float32)
    for half in range(2):
        part = pl.ds(half * chips, chips)
        left = flat(got_ref[part, :rows, :])
        own += dot_rows(left, flat(got_ref[part, rows:, :]))
        other += dot_rows(left, flat(other_ref[part, :, :]))
    own = own.astype(jnp.bfloat16)
    other = other.astype(jnp.bfloat16)
    source = lax.broadcasted_iota(jnp.int32, (cols, cols), 0)
    target = lax.broadcasted_iota(jnp.int32, (cols, cols), 1)
    seat = source % (cols // 2)
    seat_core = jnp.where(source < cols // 2, core_ref[0], 1 - core_ref[0])
    place = (seat // rows * 2 + seat_core) * rows + seat % rows
    order = jnp.where(place == target, 1.0, 0.0).astype(jnp.bfloat16)
    for half in range(2):
        span = slice(half * (size // 2), (half + 1) * (size // 2))
        both = jnp.concatenate([own[:, span], other[:, span]], axis=1)
        placed = jnp.dot(both, order, preferred_element_type=jnp.float32)
        out_ref[pl.ds(half * chips, chips), :, :] = placed.reshape(chips, rows, cols).astype(
            jnp.bfloat16
        )


def plane_blocks(core, got, other):
    blocks, rows, cols = other.shape
    return pl.pallas_call(
        plane_kernel,
        out_shape=jax.ShapeDtypeStruct((blocks, rows, cols), jnp.bfloat16),
        in_specs=[
            pl.BlockSpec(memory_space=pltpu.SMEM),
            pl.BlockSpec(memory_space=pltpu.VMEM),
            pl.BlockSpec(memory_space=pltpu.VMEM),
        ],
        out_specs=pl.BlockSpec(memory_space=pltpu.VMEM),
        compiler_params=pltpu.CompilerParams(vmem_limit_bytes=32 * 1024 * 1024),
    )(core, got, other)


def make(wide, row):
    groups = chip_groups(wide, row)

    def shards(pair, token_valid, w_pair, w_gate, w_out):
        rows_dev, cols_dev, width = pair.shape
        hidden = w_out.shape[0]
        valid = token_valid.astype(jnp.float32)
        row_valid = lax.dynamic_slice_in_dim(
            valid, lax.axis_index("wide") * rows_dev, rows_dev, 0
        )
        col_valid = lax.dynamic_slice_in_dim(valid, lax.axis_index("row") * cols_dev, cols_dev, 0)
        weight_mask = (row_valid[:, None] * col_valid[None, :]).reshape(1, -1)
        normed = normalize(pair.astype(jnp.float32), 2).astype(jnp.bfloat16)
        normed = normed.reshape(-1, width)
        proj = jnp.einsum("de,nd->en", w_pair, normed, preferred_element_type=jnp.float32)
        left = jax.nn.sigmoid(proj[:hidden]) * proj[hidden : 2 * hidden] * weight_mask
        right = jax.nn.sigmoid(proj[2 * hidden : 3 * hidden]) * proj[3 * hidden :] * weight_mask
        sent = jnp.concatenate(
            [
                left.astype(jnp.bfloat16).reshape(hidden, rows_dev, cols_dev),
                right.astype(jnp.bfloat16).reshape(hidden, rows_dev, cols_dev),
            ],
            axis=1,
        )
        got = exchange(sent, groups)
        other = lax.ppermute(
            got[:, rows_dev:, :], "wide", [(i, i ^ 1) for i in range(wide)]
        )
        core = (lax.axis_index("wide") % 2).astype(jnp.int32).reshape(1)
        plane = plane_blocks(core, got, other)
        returned = exchange(plane, groups)
        gating = jax.nn.sigmoid(
            jnp.einsum("nd,de->ne", normed, w_gate, preferred_element_type=jnp.float32)
        )
        tri_norm = normalize(returned.astype(jnp.float32), 0).astype(jnp.bfloat16)
        mixed = jnp.einsum(
            "hn,hc->nc", tri_norm.reshape(hidden, -1), w_out, preferred_element_type=jnp.float32
        )
        return (gating * mixed).astype(jnp.bfloat16).reshape(rows_dev, cols_dev, width)

    return shards


def solution(mesh):
    placed = (P("wide", "row", None), P(), P(), P(), P())
    return jax.shard_map(
        make(mesh.shape["wide"], mesh.shape["row"]),
        mesh=mesh,
        in_specs=placed,
        out_specs=P("wide", "row", None),
        check_vma=False,
    )
```

```python
import jax
import jax.numpy as jnp
from jax import lax
from jax.experimental import pallas as pl
from jax.experimental.pallas import tpu as pltpu
from jax.sharding import PartitionSpec as P


def normalize(values, axis):
    mean = jnp.mean(values, axis=axis, keepdims=True)
    centered = values - mean
    spread = jnp.mean(centered * centered, axis=axis, keepdims=True)
    return centered * lax.rsqrt(spread + 1e-05)


def chip_groups(wide, row):
    chips = wide // 2
    return [
        [(chip * 2 + core) * row + half for half in range(row) for chip in range(chips)]
        for core in range(2)
    ]


def exchange(blocks, groups):
    return lax.all_to_all(
        blocks, ("wide", "row"), split_axis=0, concat_axis=0, tiled=True, axis_index_groups=groups
    )


def dot_rows(left, right):
    return lax.dot_general(
        left, right, (((1,), (1,)), ((), ())), preferred_element_type=jnp.float32
    )


def sigmoid(values):
    return 0.5 * jnp.tanh(0.5 * values) + 0.5


def project_kernel(pair_ref, valid_ref, w_ref, sent_ref, normed_ref, held):
    rows, cols, width = pair_ref.shape
    hidden = sent_ref.shape[0]
    ones = jnp.ones((width, width), jnp.bfloat16)

    def total(values):
        return jnp.dot(values, ones, preferred_element_type=jnp.float32)

    turned = w_ref[...].T
    valid = valid_ref[...].astype(jnp.float32)
    seat = lax.broadcasted_iota(jnp.int32, valid.shape, 1)
    first = lax.axis_index("wide") * rows
    col_valid = jnp.where(lax.axis_index("row") == 0, valid[:, :cols], valid[:, cols:])
    for row in range(rows):
        row_valid = jnp.sum(jnp.where(seat == first + row, valid, 0.0), axis=1, keepdims=True)
        mask = row_valid * col_valid
        values = pair_ref[row]
        centered = values.astype(jnp.float32) - total(values) * (1.0 / width)
        square = centered * centered
        high = square.astype(jnp.bfloat16)
        low = (square - high.astype(jnp.float32)).astype(jnp.bfloat16)
        spread = (total(high) + total(low)) * (1.0 / width)
        normed = (centered * lax.rsqrt(spread + 1e-05)).astype(jnp.bfloat16)
        normed_ref[pl.ds(row * cols, cols), :] = normed
        proj = dot_rows(turned, normed)
        held[row] = sigmoid(proj[:hidden]) * proj[hidden : 2 * hidden] * mask
        held[rows + row] = sigmoid(proj[2 * hidden : 3 * hidden]) * proj[3 * hidden :] * mask
    step = 16
    for first_channel in range(0, hidden, step):
        part = slice(first_channel, first_channel + step)
        sent_ref[part] = jnp.transpose(held[:, part, :], (1, 0, 2)).astype(jnp.bfloat16)


def project_blocks(pair, token_valid, w_pair):
    rows, cols, width = pair.shape
    hidden = w_pair.shape[1] // 4
    return pl.pallas_call(
        project_kernel,
        out_shape=(
            jax.ShapeDtypeStruct((hidden, 2 * rows, cols), jnp.bfloat16),
            jax.ShapeDtypeStruct((rows * cols, width), jnp.bfloat16),
        ),
        in_specs=[pl.BlockSpec(memory_space=pltpu.VMEM)] * 3,
        out_specs=(pl.BlockSpec(memory_space=pltpu.VMEM),) * 2,
        scratch_shapes=[pltpu.VMEM((2 * rows, hidden, cols), jnp.float32)],
        compiler_params=pltpu.CompilerParams(vmem_limit_bytes=32 * 1024 * 1024),
    )(pair, token_valid.reshape(1, -1), w_pair)


def plane_kernel(got_ref, other_ref, out_ref):
    blocks, rows, cols = out_ref.shape
    chips = blocks // 2
    size = chips * rows

    def flat(values):
        return values.astype(jnp.float32).reshape(size, cols).astype(jnp.bfloat16)

    own = jnp.zeros((size, size), jnp.float32)
    other = jnp.zeros((size, size), jnp.float32)
    for half in range(2):
        part = pl.ds(half * chips, chips)
        left = flat(got_ref[part, :rows, :])
        own += dot_rows(left, flat(got_ref[part, rows:, :]))
        other += dot_rows(left, flat(other_ref[part, :, :]))
    own = own.astype(jnp.bfloat16)
    other = other.astype(jnp.bfloat16)
    core = lax.axis_index("wide") % 2
    source = lax.broadcasted_iota(jnp.int32, (cols, cols), 0)
    target = lax.broadcasted_iota(jnp.int32, (cols, cols), 1)
    seat = source % (cols // 2)
    seat_core = jnp.where(source < cols // 2, core, 1 - core)
    place = (seat // rows * 2 + seat_core) * rows + seat % rows
    order = jnp.where(place == target, 1.0, 0.0).astype(jnp.bfloat16)
    for half in range(2):
        span = slice(half * (size // 2), (half + 1) * (size // 2))
        both = jnp.concatenate([own[:, span], other[:, span]], axis=1)
        placed = jnp.dot(both, order, preferred_element_type=jnp.float32)
        out_ref[pl.ds(half * chips, chips), :, :] = placed.reshape(chips, rows, cols).astype(
            jnp.bfloat16
        )


def plane_blocks(got, other):
    blocks, rows, cols = other.shape
    return pl.pallas_call(
        plane_kernel,
        out_shape=jax.ShapeDtypeStruct((blocks, rows, cols), jnp.bfloat16),
        in_specs=[
            pl.BlockSpec(memory_space=pltpu.VMEM),
            pl.BlockSpec(memory_space=pltpu.VMEM),
        ],
        out_specs=pl.BlockSpec(memory_space=pltpu.VMEM),
        compiler_params=pltpu.CompilerParams(vmem_limit_bytes=32 * 1024 * 1024),
    )(got, other)


def make(wide, row):
    groups = chip_groups(wide, row)

    def shards(pair, token_valid, w_pair, w_gate, w_out):
        rows_dev, cols_dev, width = pair.shape
        hidden = w_out.shape[0]
        sent, normed = project_blocks(pair, token_valid, w_pair)
        got = exchange(sent, groups)
        other = lax.ppermute(
            got[:, rows_dev:, :], "wide", [(i, i ^ 1) for i in range(wide)]
        )
        plane = plane_blocks(got, other)
        returned = exchange(plane, groups)
        gating = jax.nn.sigmoid(
            jnp.einsum("nd,de->ne", normed, w_gate, preferred_element_type=jnp.float32)
        )
        tri_norm = normalize(returned.astype(jnp.float32), 0).astype(jnp.bfloat16)
        mixed = jnp.einsum(
            "hn,hc->nc", tri_norm.reshape(hidden, -1), w_out, preferred_element_type=jnp.float32
        )
        return (gating * mixed).astype(jnp.bfloat16).reshape(rows_dev, cols_dev, width)

    return shards


def solution(mesh):
    placed = (P("wide", "row", None), P(), P(), P(), P())
    return jax.shard_map(
        make(mesh.shape["wide"], mesh.shape["row"]),
        mesh=mesh,
        in_specs=placed,
        out_specs=P("wide", "row", None),
        check_vma=False,
    )
```

```python
import jax
import jax.numpy as jnp
from jax import lax
from jax.experimental import pallas as pl
from jax.experimental.pallas import tpu as pltpu
from jax.sharding import PartitionSpec as P

VMEM = pl.BlockSpec(memory_space=pltpu.VMEM)
ANY = pl.BlockSpec(memory_space=pl.ANY)


def chip_groups(wide, row):
    chips = wide // 2
    return [
        [(chip * 2 + core) * row + half for half in range(row) for chip in range(chips)]
        for core in range(2)
    ]


def exchange(blocks, groups):
    return lax.all_to_all(
        blocks, ("wide", "row"), split_axis=0, concat_axis=0, tiled=True, axis_index_groups=groups
    )


def dot_rows(left, right):
    return lax.dot_general(
        left, right, (((1,), (1,)), ((), ())), preferred_element_type=jnp.float32
    )


def sigmoid(values):
    return 0.5 * jnp.tanh(0.5 * values) + 0.5


def project_kernel(
    pair_hbm, valid_hbm, w_hbm, gate_hbm, out_hbm,
    sent_ref, normed_ref, gate_ref, out_ref,
    pair_ref, valid_ref, w_ref, held, arrived,
):
    rows, cols, width = pair_ref.shape
    hidden = sent_ref.shape[0]
    pieces = [(w_hbm, w_ref)]
    pieces += [(pair_hbm.at[row], pair_ref.at[row]) for row in range(rows)]
    pieces += [(valid_hbm, valid_ref), (gate_hbm, gate_ref), (out_hbm, out_ref)]
    copies = [
        pltpu.make_async_copy(source, target, arrived.at[index])
        for index, (source, target) in enumerate(pieces)
    ]
    for copy in copies:
        copy.start()
    ones = jnp.ones((width, width), jnp.bfloat16)

    def total(values):
        return jnp.dot(values, ones, preferred_element_type=jnp.float32)

    copies[0].wait()
    turned = w_ref[...].T
    copies[rows + 1].wait()
    valid = valid_ref[...].astype(jnp.float32)
    seat = lax.broadcasted_iota(jnp.int32, valid.shape, 1)
    first = lax.axis_index("wide") * rows
    col_valid = jnp.where(lax.axis_index("row") == 0, valid[:, :cols], valid[:, cols:])
    for row in range(rows):
        row_valid = jnp.sum(jnp.where(seat == first + row, valid, 0.0), axis=1, keepdims=True)
        mask = row_valid * col_valid
        copies[1 + row].wait()
        values = pair_ref[row]
        centered = values.astype(jnp.float32) - total(values) * (1.0 / width)
        square = centered * centered
        high = square.astype(jnp.bfloat16)
        low = (square - high.astype(jnp.float32)).astype(jnp.bfloat16)
        spread = (total(high) + total(low)) * (1.0 / width)
        normed = (centered * lax.rsqrt(spread + 1e-05)).astype(jnp.bfloat16)
        normed_ref[pl.ds(row * cols, cols), :] = normed
        proj = dot_rows(turned, normed)
        held[row] = sigmoid(proj[:hidden]) * proj[hidden : 2 * hidden] * mask
        held[rows + row] = sigmoid(proj[2 * hidden : 3 * hidden]) * proj[3 * hidden :] * mask
    step = 16
    for first_channel in range(0, hidden, step):
        part = slice(first_channel, first_channel + step)
        sent_ref[part] = jnp.transpose(held[:, part, :], (1, 0, 2)).astype(jnp.bfloat16)
    copies[rows + 2].wait()
    copies[rows + 3].wait()


def project_blocks(pair, token_valid, w_pair, w_gate, w_out):
    rows, cols, width = pair.shape
    hidden = w_out.shape[0]
    valid = token_valid.reshape(1, -1)
    return pl.pallas_call(
        project_kernel,
        out_shape=(
            jax.ShapeDtypeStruct((hidden, 2 * rows, cols), jnp.bfloat16),
            jax.ShapeDtypeStruct((rows * cols, width), jnp.bfloat16),
            jax.ShapeDtypeStruct(w_gate.shape, jnp.bfloat16),
            jax.ShapeDtypeStruct(w_out.shape, jnp.bfloat16),
        ),
        in_specs=[ANY] * 5,
        out_specs=(VMEM,) * 4,
        scratch_shapes=[
            pltpu.VMEM(pair.shape, jnp.bfloat16),
            pltpu.VMEM(valid.shape, jnp.int32),
            pltpu.VMEM(w_pair.shape, jnp.bfloat16),
            pltpu.VMEM((2 * rows, hidden, cols), jnp.float32),
            pltpu.SemaphoreType.DMA((rows + 4,)),
        ],
    )(pair, valid, w_pair, w_gate, w_out)


def flat(values):
    chips, rows, cols = values.shape
    return values.astype(jnp.float32).reshape(chips * rows, cols).astype(jnp.bfloat16)


def column_order(core, rows, cols):
    source = lax.broadcasted_iota(jnp.int32, (cols // 2, cols), 0)
    target = lax.broadcasted_iota(jnp.int32, (cols // 2, cols), 1)
    place = (source // rows * 2 + core) * rows + source % rows
    return jnp.where(place == target, 1.0, 0.0).astype(jnp.bfloat16)


def own_kernel(got_ref, normed_ref, gate_ref, left_ref, own_ref, gating_ref):
    blocks, both, cols = got_ref.shape
    rows, chips = both // 2, blocks // 2
    size = chips * rows
    own = jnp.zeros((size, size), jnp.float32)
    for half in range(2):
        part = pl.ds(half * chips, chips)
        left = flat(got_ref[part, :rows, :])
        left_ref[half] = left
        own += dot_rows(left, flat(got_ref[part, rows:, :]))
    own = own.astype(jnp.bfloat16)
    order = column_order(lax.axis_index("wide") % 2, rows, cols)
    for half in range(2):
        span = slice(half * (size // 2), (half + 1) * (size // 2))
        own_ref[half] = jnp.dot(own[:, span], order, preferred_element_type=jnp.float32)
    gating_ref[...] = sigmoid(
        jnp.dot(normed_ref[...], gate_ref[...], preferred_element_type=jnp.float32)
    )


def own_part(got, normed, w_gate):
    blocks, both, cols = got.shape
    size = blocks // 2 * (both // 2)
    return pl.pallas_call(
        own_kernel,
        out_shape=(
            jax.ShapeDtypeStruct((2, size, cols), jnp.bfloat16),
            jax.ShapeDtypeStruct((2, size, cols), jnp.float32),
            jax.ShapeDtypeStruct(normed.shape, jnp.float32),
        ),
        in_specs=[VMEM] * 3,
        out_specs=(VMEM,) * 3,
        cost_estimate=pl.CostEstimate(
            flops=4 * size * size * cols, bytes_accessed=3 * 1024 * 1024, transcendentals=0
        ),
    )(got, normed, w_gate)


def plane_kernel(other_ref, left_ref, own_ref, out_ref):
    blocks, rows, cols = out_ref.shape
    chips = blocks // 2
    size = chips * rows
    other = jnp.zeros((size, size), jnp.float32)
    for half in range(2):
        other += dot_rows(left_ref[half], flat(other_ref[pl.ds(half * chips, chips)]))
    other = other.astype(jnp.bfloat16)
    order = column_order(1 - lax.axis_index("wide") % 2, rows, cols)
    for half in range(2):
        span = slice(half * (size // 2), (half + 1) * (size // 2))
        placed = own_ref[half] + jnp.dot(
            other[:, span], order, preferred_element_type=jnp.float32
        )
        out_ref[pl.ds(half * chips, chips)] = placed.reshape(chips, rows, cols).astype(
            jnp.bfloat16
        )


def plane_blocks(other, left, own):
    return pl.pallas_call(
        plane_kernel,
        out_shape=jax.ShapeDtypeStruct(other.shape, jnp.bfloat16),
        in_specs=[VMEM] * 3,
        out_specs=VMEM,
    )(other, left, own)


def finish_kernel(returned_ref, gating_ref, out_ref, update_hbm, staged, left_device):
    rows, cols, width = staged.shape
    hidden = returned_ref.shape[0]
    turned = jnp.transpose(returned_ref[...].astype(jnp.float32), (1, 0, 2))
    copies = []
    for row in range(rows):
        values = turned[row]
        mean = jnp.sum(values, axis=0, keepdims=True) * (1.0 / hidden)
        centered = values - mean
        spread = jnp.sum(centered * centered, axis=0, keepdims=True) * (1.0 / hidden)
        tri_norm = (centered * lax.rsqrt(spread + 1e-05)).astype(jnp.bfloat16)
        mixed = lax.dot_general(
            tri_norm, out_ref[...], (((0,), (0,)), ((), ())), preferred_element_type=jnp.float32
        )
        staged[row] = (gating_ref[pl.ds(row * cols, cols), :] * mixed).astype(jnp.bfloat16)
        copy = pltpu.make_async_copy(staged.at[row], update_hbm.at[row], left_device.at[row])
        copy.start()
        copies.append(copy)
    for copy in copies:
        copy.wait()


def finish(returned, gating, w_out, shape):
    return pl.pallas_call(
        finish_kernel,
        out_shape=jax.ShapeDtypeStruct(shape, jnp.bfloat16),
        in_specs=[VMEM] * 3,
        out_specs=ANY,
        scratch_shapes=[
            pltpu.VMEM(shape, jnp.bfloat16),
            pltpu.SemaphoreType.DMA((shape[0],)),
        ],
    )(returned, gating, w_out)


def make(wide, row):
    groups = chip_groups(wide, row)

    def shards(pair, token_valid, w_pair, w_gate, w_out):
        rows = pair.shape[0]
        sent, normed, w_gate, w_out = project_blocks(pair, token_valid, w_pair, w_gate, w_out)
        got = exchange(sent, groups)
        other = lax.ppermute(got[:, rows:, :], "wide", [(i, i ^ 1) for i in range(wide)])
        left, own, gating = own_part(got, normed, w_gate)
        returned = exchange(plane_blocks(other, left, own), groups)
        return finish(returned, gating, w_out, pair.shape)

    return shards


def solution(mesh):
    placed = (P("wide", "row", None), P(), P(), P(), P())
    return jax.shard_map(
        make(mesh.shape["wide"], mesh.shape["row"]),
        mesh=mesh,
        in_specs=placed,
        out_specs=P("wide", "row", None),
        check_vma=False,
    )
```

```python
import jax
import jax.numpy as jnp
from jax import lax
from jax.experimental import pallas as pl
from jax.experimental.pallas import tpu as pltpu
from jax.sharding import PartitionSpec as P

VMEM = pl.BlockSpec(memory_space=pltpu.VMEM)
ANY = pl.BlockSpec(memory_space=pl.ANY)
ROOM = pltpu.CompilerParams(vmem_limit_bytes=32 * 1024 * 1024)


def chip_groups(wide, row):
    chips = wide // 2
    return [
        [(chip * 2 + core) * row + half for half in range(row) for chip in range(chips)]
        for core in range(2)
    ]


def exchange(blocks, groups):
    return lax.all_to_all(
        blocks, ("wide", "row"), split_axis=0, concat_axis=0, tiled=True, axis_index_groups=groups
    )


def dot_rows(left, right):
    return lax.dot_general(
        left, right, (((1,), (1,)), ((), ())), preferred_element_type=jnp.float32
    )


def sigmoid(values):
    return 0.5 * jnp.tanh(0.5 * values) + 0.5


def normed_kernel(pair_ref, normed_ref):
    rows, cols, width = pair_ref.shape
    ones = jnp.ones((width, width), jnp.bfloat16)

    def total(values):
        return jnp.dot(values, ones, preferred_element_type=jnp.float32)

    for row in range(rows):
        values = pair_ref[row]
        centered = values.astype(jnp.float32) - total(values) * (1.0 / width)
        square = centered * centered
        high = square.astype(jnp.bfloat16)
        low = (square - high.astype(jnp.float32)).astype(jnp.bfloat16)
        spread = (total(high) + total(low)) * (1.0 / width)
        normed_ref[pl.ds(row * cols, cols), :] = (
            centered * lax.rsqrt(spread + 1e-05)
        ).astype(jnp.bfloat16)


def norm_pair(pair):
    rows, cols, width = pair.shape
    return pl.pallas_call(
        normed_kernel,
        out_shape=jax.ShapeDtypeStruct((rows * cols, width), jnp.bfloat16),
        in_specs=[VMEM],
        out_specs=VMEM,
        compiler_params=ROOM,
        cost_estimate=pl.CostEstimate(
            flops=8 * rows * cols * width * width, bytes_accessed=4 * 1024 * 1024, transcendentals=0
        ),
    )(pair)


def project_kernel(normed_ref, valid_ref, w_ref, sent_ref, held):
    hidden, both, cols = sent_ref.shape
    rows = both // 2
    turned = w_ref[...].T
    valid = valid_ref[...].astype(jnp.float32)
    seat = lax.broadcasted_iota(jnp.int32, valid.shape, 1)
    first = lax.axis_index("wide") * rows
    col_valid = jnp.where(lax.axis_index("row") == 0, valid[:, :cols], valid[:, cols:])
    for row in range(rows):
        row_valid = jnp.sum(jnp.where(seat == first + row, valid, 0.0), axis=1, keepdims=True)
        mask = row_valid * col_valid
        proj = dot_rows(turned, normed_ref[pl.ds(row * cols, cols), :])
        held[row] = sigmoid(proj[:hidden]) * proj[hidden : 2 * hidden] * mask
        held[rows + row] = sigmoid(proj[2 * hidden : 3 * hidden]) * proj[3 * hidden :] * mask
    step = 16
    for first_channel in range(0, hidden, step):
        part = slice(first_channel, first_channel + step)
        sent_ref[part] = jnp.transpose(held[:, part, :], (1, 0, 2)).astype(jnp.bfloat16)


def project_blocks(normed, token_valid, w_pair, rows, hidden):
    cols = normed.shape[0] // rows
    return pl.pallas_call(
        project_kernel,
        out_shape=jax.ShapeDtypeStruct((hidden, 2 * rows, cols), jnp.bfloat16),
        in_specs=[VMEM] * 3,
        out_specs=VMEM,
        scratch_shapes=[pltpu.VMEM((2 * rows, hidden, cols), jnp.float32)],
        compiler_params=ROOM,
    )(normed, token_valid.reshape(1, -1), w_pair)


def flat(values):
    chips, rows, cols = values.shape
    return values.astype(jnp.float32).reshape(chips * rows, cols).astype(jnp.bfloat16)


def column_order(core, rows, cols):
    source = lax.broadcasted_iota(jnp.int32, (cols // 2, cols), 0)
    target = lax.broadcasted_iota(jnp.int32, (cols // 2, cols), 1)
    place = (source // rows * 2 + core) * rows + source % rows
    return jnp.where(place == target, 1.0, 0.0).astype(jnp.bfloat16)


def own_kernel(
    got_ref, normed_ref, gate_ref, w_out_ref, left_ref, own_ref, gating_ref, held_out_ref
):
    held_out_ref[...] = w_out_ref[...]
    blocks, both, cols = got_ref.shape
    rows, chips = both // 2, blocks // 2
    size = chips * rows
    own = jnp.zeros((size, size), jnp.float32)
    for half in range(2):
        part = pl.ds(half * chips, chips)
        left = flat(got_ref[part, :rows, :])
        left_ref[half] = left
        own += dot_rows(left, flat(got_ref[part, rows:, :]))
    own = own.astype(jnp.bfloat16)
    order = column_order(lax.axis_index("wide") % 2, rows, cols)
    for half in range(2):
        span = slice(half * (size // 2), (half + 1) * (size // 2))
        own_ref[half] = jnp.dot(own[:, span], order, preferred_element_type=jnp.float32)
    gating_ref[...] = sigmoid(
        jnp.dot(normed_ref[...], gate_ref[...], preferred_element_type=jnp.float32)
    )


def own_part(got, normed, w_gate, w_out):
    blocks, both, cols = got.shape
    size = blocks // 2 * (both // 2)
    return pl.pallas_call(
        own_kernel,
        out_shape=(
            jax.ShapeDtypeStruct((2, size, cols), jnp.bfloat16),
            jax.ShapeDtypeStruct((2, size, cols), jnp.float32),
            jax.ShapeDtypeStruct(normed.shape, jnp.float32),
            jax.ShapeDtypeStruct(w_out.shape, jnp.bfloat16),
        ),
        in_specs=[VMEM] * 4,
        out_specs=(VMEM,) * 4,
        compiler_params=ROOM,
        cost_estimate=pl.CostEstimate(
            flops=4 * size * size * cols, bytes_accessed=3 * 1024 * 1024, transcendentals=0
        ),
    )(got, normed, w_gate, w_out)


def plane_kernel(other_ref, left_ref, own_ref, out_ref):
    blocks, rows, cols = out_ref.shape
    chips = blocks // 2
    size = chips * rows
    other = jnp.zeros((size, size), jnp.float32)
    for half in range(2):
        other += dot_rows(left_ref[half], flat(other_ref[pl.ds(half * chips, chips)]))
    other = other.astype(jnp.bfloat16)
    order = column_order(1 - lax.axis_index("wide") % 2, rows, cols)
    for half in range(2):
        span = slice(half * (size // 2), (half + 1) * (size // 2))
        placed = own_ref[half] + jnp.dot(
            other[:, span], order, preferred_element_type=jnp.float32
        )
        out_ref[pl.ds(half * chips, chips)] = placed.reshape(chips, rows, cols).astype(
            jnp.bfloat16
        )


def plane_blocks(other, left, own):
    return pl.pallas_call(
        plane_kernel,
        out_shape=jax.ShapeDtypeStruct(other.shape, jnp.bfloat16),
        in_specs=[VMEM] * 3,
        out_specs=VMEM,
        compiler_params=ROOM,
    )(other, left, own)


def finish_kernel(returned_ref, gating_ref, out_ref, update_hbm, staged, left_device):
    rows, cols, width = staged.shape
    hidden = returned_ref.shape[0]
    turned = jnp.transpose(returned_ref[...].astype(jnp.float32), (1, 0, 2))
    copies = []
    for row in range(rows):
        values = turned[row]
        mean = jnp.sum(values, axis=0, keepdims=True) * (1.0 / hidden)
        centered = values - mean
        spread = jnp.sum(centered * centered, axis=0, keepdims=True) * (1.0 / hidden)
        tri_norm = (centered * lax.rsqrt(spread + 1e-05)).astype(jnp.bfloat16)
        mixed = lax.dot_general(
            tri_norm, out_ref[...], (((0,), (0,)), ((), ())), preferred_element_type=jnp.float32
        )
        staged[row] = (gating_ref[pl.ds(row * cols, cols), :] * mixed).astype(jnp.bfloat16)
        copy = pltpu.make_async_copy(staged.at[row], update_hbm.at[row], left_device.at[row])
        copy.start()
        copies.append(copy)
    for copy in copies:
        copy.wait()


def finish(returned, gating, w_out, shape):
    return pl.pallas_call(
        finish_kernel,
        out_shape=jax.ShapeDtypeStruct(shape, jnp.bfloat16),
        in_specs=[VMEM] * 3,
        out_specs=ANY,
        scratch_shapes=[
            pltpu.VMEM(shape, jnp.bfloat16),
            pltpu.SemaphoreType.DMA((shape[0],)),
        ],
        compiler_params=ROOM,
    )(returned, gating, w_out)


def make(wide, row):
    groups = chip_groups(wide, row)

    def shards(pair, token_valid, w_pair, w_gate, w_out):
        rows = pair.shape[0]
        normed = norm_pair(pair)
        sent = project_blocks(normed, token_valid, w_pair, rows, w_out.shape[0])
        got = exchange(sent, groups)
        other = lax.ppermute(got[:, rows:, :], "wide", [(i, i ^ 1) for i in range(wide)])
        left, own, gating, w_out = own_part(got, normed, w_gate, w_out)
        returned = exchange(plane_blocks(other, left, own), groups)
        return finish(returned, gating, w_out, pair.shape)

    return shards


def solution(mesh):
    placed = (P("wide", "row", None), P(), P(), P(), P())
    return jax.shard_map(
        make(mesh.shape["wide"], mesh.shape["row"]),
        mesh=mesh,
        in_specs=placed,
        out_specs=P("wide", "row", None),
        check_vma=False,
    )
```

```python
import functools

import jax
import jax.numpy as jnp
from jax import lax
from jax.experimental import pallas as pl
from jax.experimental.pallas import tpu as pltpu
from jax.sharding import PartitionSpec as P

VMEM = pl.BlockSpec(memory_space=pltpu.VMEM)
ANY = pl.BlockSpec(memory_space=pl.ANY)
ROOM = pltpu.CompilerParams(vmem_limit_bytes=32 * 1024 * 1024)


Y, Z, X = 4, 8, 4
LEAD = (2, 5, 2)


def group_order(chips, row):
    def place(number):
        half, chip = divmod(number, chips)
        x_in = X // row
        return chip // (x_in * Z), chip // x_in % Z, half * x_in + chip % x_in

    def apart(number):
        y, z, x = place(number)
        along = abs(z - LEAD[1])
        return abs(y - LEAD[0]) + min(along, Z - along) + abs(x - LEAD[2])

    return sorted(range(row * chips), key=lambda number: (apart(number) > 0, -apart(number)))


def chip_groups(order, row):
    chips = len(order) // row
    return [
        [(number % chips * 2 + core) * row + number // chips for number in order]
        for core in range(2)
    ]


def exchange(blocks, groups):
    return lax.all_to_all(
        blocks, ("wide", "row"), split_axis=0, concat_axis=0, tiled=True, axis_index_groups=groups
    )


def dot_rows(left, right):
    return lax.dot_general(
        left, right, (((1,), (1,)), ((), ())), preferred_element_type=jnp.float32
    )


def sigmoid(values):
    return 0.5 * jnp.tanh(0.5 * values) + 0.5


def normed_kernel(pair_ref, normed_ref):
    rows, cols, width = pair_ref.shape
    ones = jnp.ones((width, width), jnp.bfloat16)

    def total(values):
        return jnp.dot(values, ones, preferred_element_type=jnp.float32)

    for row in range(rows):
        values = pair_ref[row]
        centered = values.astype(jnp.float32) - total(values) * (1.0 / width)
        square = centered * centered
        high = square.astype(jnp.bfloat16)
        low = (square - high.astype(jnp.float32)).astype(jnp.bfloat16)
        spread = (total(high) + total(low)) * (1.0 / width)
        normed_ref[pl.ds(row * cols, cols), :] = (
            centered * lax.rsqrt(spread + 1e-05)
        ).astype(jnp.bfloat16)


def norm_pair(pair):
    rows, cols, width = pair.shape
    return pl.pallas_call(
        normed_kernel,
        out_shape=jax.ShapeDtypeStruct((rows * cols, width), jnp.bfloat16),
        in_specs=[VMEM],
        out_specs=VMEM,
        compiler_params=ROOM,
        cost_estimate=pl.CostEstimate(
            flops=8 * rows * cols * width * width, bytes_accessed=4 * 1024 * 1024, transcendentals=0
        ),
    )(pair)


def project_kernel(normed_ref, valid_ref, w_ref, sent_ref, held):
    hidden, both, cols = sent_ref.shape
    rows = both // 2
    turned = w_ref[...].T
    valid = valid_ref[...].astype(jnp.float32)
    seat = lax.broadcasted_iota(jnp.int32, valid.shape, 1)
    first = lax.axis_index("wide") * rows
    col_valid = jnp.where(lax.axis_index("row") == 0, valid[:, :cols], valid[:, cols:])
    for row in range(rows):
        row_valid = jnp.sum(jnp.where(seat == first + row, valid, 0.0), axis=1, keepdims=True)
        mask = row_valid * col_valid
        proj = dot_rows(turned, normed_ref[pl.ds(row * cols, cols), :])
        held[row] = sigmoid(proj[:hidden]) * proj[hidden : 2 * hidden] * mask
        held[rows + row] = sigmoid(proj[2 * hidden : 3 * hidden]) * proj[3 * hidden :] * mask
    step = 16
    for first_channel in range(0, hidden, step):
        part = slice(first_channel, first_channel + step)
        sent_ref[part] = jnp.transpose(held[:, part, :], (1, 0, 2)).astype(jnp.bfloat16)


def project_blocks(normed, token_valid, w_pair, rows, hidden):
    cols = normed.shape[0] // rows
    return pl.pallas_call(
        project_kernel,
        out_shape=jax.ShapeDtypeStruct((hidden, 2 * rows, cols), jnp.bfloat16),
        in_specs=[VMEM] * 3,
        out_specs=VMEM,
        scratch_shapes=[pltpu.VMEM((2 * rows, hidden, cols), jnp.float32)],
        compiler_params=ROOM,
    )(normed, token_valid.reshape(1, -1), w_pair)


def flat(values):
    chips, rows, cols = values.shape
    return values.astype(jnp.float32).reshape(chips * rows, cols).astype(jnp.bfloat16)


def column_order(core, rows, cols):
    source = lax.broadcasted_iota(jnp.int32, (cols // 2, cols), 0)
    target = lax.broadcasted_iota(jnp.int32, (cols // 2, cols), 1)
    place = (source // rows * 2 + core) * rows + source % rows
    return jnp.where(place == target, 1.0, 0.0).astype(jnp.bfloat16)


def own_kernel(
    seats, got_ref, normed_ref, gate_ref, w_out_ref, left_ref, own_ref, gating_ref, held_out_ref
):
    held_out_ref[...] = w_out_ref[...]
    blocks, both, cols = got_ref.shape
    rows, chips = both // 2, blocks // 2
    size = chips * rows
    own = jnp.zeros((size, size), jnp.float32)
    for half in range(2):
        got = jnp.stack([got_ref[seat] for seat in seats[half * chips : (half + 1) * chips]])
        left = flat(got[:, :rows, :])
        left_ref[half] = left
        own += dot_rows(left, flat(got[:, rows:, :]))
    own = own.astype(jnp.bfloat16)
    order = column_order(lax.axis_index("wide") % 2, rows, cols)
    for half in range(2):
        span = slice(half * (size // 2), (half + 1) * (size // 2))
        own_ref[half] = jnp.dot(own[:, span], order, preferred_element_type=jnp.float32)
    gating_ref[...] = sigmoid(
        jnp.dot(normed_ref[...], gate_ref[...], preferred_element_type=jnp.float32)
    )


def own_part(seats, got, normed, w_gate, w_out):
    blocks, both, cols = got.shape
    size = blocks // 2 * (both // 2)
    return pl.pallas_call(
        functools.partial(own_kernel, seats),
        out_shape=(
            jax.ShapeDtypeStruct((2, size, cols), jnp.bfloat16),
            jax.ShapeDtypeStruct((2, size, cols), jnp.float32),
            jax.ShapeDtypeStruct(normed.shape, jnp.float32),
            jax.ShapeDtypeStruct(w_out.shape, jnp.bfloat16),
        ),
        in_specs=[VMEM] * 4,
        out_specs=(VMEM,) * 4,
        compiler_params=ROOM,
        cost_estimate=pl.CostEstimate(
            flops=4 * size * size * cols, bytes_accessed=3 * 1024 * 1024, transcendentals=0
        ),
    )(got, normed, w_gate, w_out)


def plane_kernel(seats, other_ref, left_ref, own_ref, out_ref):
    blocks, rows, cols = out_ref.shape
    chips = blocks // 2
    size = chips * rows
    other = jnp.zeros((size, size), jnp.float32)
    for half in range(2):
        part = seats[half * chips : (half + 1) * chips]
        other += dot_rows(left_ref[half], flat(jnp.stack([other_ref[seat] for seat in part])))
    other = other.astype(jnp.bfloat16)
    order = column_order(1 - lax.axis_index("wide") % 2, rows, cols)
    for half in range(2):
        span = slice(half * (size // 2), (half + 1) * (size // 2))
        placed = own_ref[half] + jnp.dot(
            other[:, span], order, preferred_element_type=jnp.float32
        )
        blocks_back = placed.reshape(chips, rows, cols).astype(jnp.bfloat16)
        for chip in range(chips):
            out_ref[seats[half * chips + chip]] = blocks_back[chip]


def plane_blocks(seats, other, left, own):
    return pl.pallas_call(
        functools.partial(plane_kernel, seats),
        out_shape=jax.ShapeDtypeStruct(other.shape, jnp.bfloat16),
        in_specs=[VMEM] * 3,
        out_specs=VMEM,
        compiler_params=ROOM,
    )(other, left, own)


def finish_kernel(returned_ref, gating_ref, out_ref, update_hbm, staged, left_device):
    rows, cols, width = staged.shape
    hidden = returned_ref.shape[0]
    turned = jnp.transpose(returned_ref[...].astype(jnp.float32), (1, 0, 2))
    copies = []
    for row in range(rows):
        values = turned[row]
        mean = jnp.sum(values, axis=0, keepdims=True) * (1.0 / hidden)
        centered = values - mean
        spread = jnp.sum(centered * centered, axis=0, keepdims=True) * (1.0 / hidden)
        tri_norm = (centered * lax.rsqrt(spread + 1e-05)).astype(jnp.bfloat16)
        mixed = lax.dot_general(
            tri_norm, out_ref[...], (((0,), (0,)), ((), ())), preferred_element_type=jnp.float32
        )
        staged[row] = (gating_ref[pl.ds(row * cols, cols), :] * mixed).astype(jnp.bfloat16)
        copy = pltpu.make_async_copy(staged.at[row], update_hbm.at[row], left_device.at[row])
        copy.start()
        copies.append(copy)
    for copy in copies:
        copy.wait()


def finish(returned, gating, w_out, shape):
    return pl.pallas_call(
        finish_kernel,
        out_shape=jax.ShapeDtypeStruct(shape, jnp.bfloat16),
        in_specs=[VMEM] * 3,
        out_specs=ANY,
        scratch_shapes=[
            pltpu.VMEM(shape, jnp.bfloat16),
            pltpu.SemaphoreType.DMA((shape[0],)),
        ],
        compiler_params=ROOM,
    )(returned, gating, w_out)


def make(wide, row):
    order = group_order(wide // 2, row)
    groups = chip_groups(order, row)
    seats = [order.index(number) for number in range(len(order))]

    def shards(pair, token_valid, w_pair, w_gate, w_out):
        rows = pair.shape[0]
        normed = norm_pair(pair)
        sent = project_blocks(normed, token_valid, w_pair, rows, w_out.shape[0])
        got = exchange(sent, groups)
        other = lax.ppermute(got[:, rows:, :], "wide", [(i, i ^ 1) for i in range(wide)])
        left, own, gating, w_out = own_part(seats, got, normed, w_gate, w_out)
        returned = exchange(plane_blocks(seats, other, left, own), groups)
        return finish(returned, gating, w_out, pair.shape)

    return shards


def solution(mesh):
    placed = (P("wide", "row", None), P(), P(), P(), P())
    return jax.shard_map(
        make(mesh.shape["wide"], mesh.shape["row"]),
        mesh=mesh,
        in_specs=placed,
        out_specs=P("wide", "row", None),
        check_vma=False,
    )
```

```python
import functools

import jax
import jax.numpy as jnp
from jax import lax
from jax.experimental import pallas as pl
from jax.experimental.pallas import tpu as pltpu
from jax.sharding import PartitionSpec as P

VMEM = pl.BlockSpec(memory_space=pltpu.VMEM)
ANY = pl.BlockSpec(memory_space=pl.ANY)
ROOM = pltpu.CompilerParams(vmem_limit_bytes=32 * 1024 * 1024)


Y, Z, X = 4, 8, 4
LEAD = (2, 5, 2)


def group_order(chips, row):
    def place(number):
        half, chip = divmod(number, chips)
        x_in = X // row
        return chip // (x_in * Z), chip // x_in % Z, half * x_in + chip % x_in

    def apart(number):
        y, z, x = place(number)
        along = abs(z - LEAD[1])
        return abs(y - LEAD[0]) + min(along, Z - along) + abs(x - LEAD[2])

    return sorted(range(row * chips), key=lambda number: (apart(number) > 0, -apart(number)))


def chip_groups(order, row):
    chips = len(order) // row
    return [
        [(number % chips * 2 + core) * row + number // chips for number in order]
        for core in range(2)
    ]


def exchange(blocks, groups):
    return lax.all_to_all(
        blocks, ("wide", "row"), split_axis=0, concat_axis=0, tiled=True, axis_index_groups=groups
    )


def dot_rows(left, right):
    return lax.dot_general(
        left, right, (((1,), (1,)), ((), ())), preferred_element_type=jnp.float32
    )


def sigmoid(values):
    return 0.5 * jnp.tanh(0.5 * values) + 0.5


def normed_kernel(pair_ref, normed_ref):
    rows, cols, width = pair_ref.shape
    share = jnp.full((2 * width, width), 1.0 / width, jnp.bfloat16)

    def mean(values):
        return jnp.dot(values, share[: values.shape[1]], preferred_element_type=jnp.float32)

    for row in range(rows):
        values = pair_ref[row]
        centered = values.astype(jnp.float32) - mean(values)
        square = centered * centered
        high = square.astype(jnp.bfloat16)
        low = (square - high.astype(jnp.float32)).astype(jnp.bfloat16)
        spread = mean(jnp.concatenate([high, low], axis=1))
        normed_ref[pl.ds(row * cols, cols), :] = (
            centered * lax.rsqrt(spread + 1e-05)
        ).astype(jnp.bfloat16)


def norm_pair(pair):
    rows, cols, width = pair.shape
    return pl.pallas_call(
        normed_kernel,
        out_shape=jax.ShapeDtypeStruct((rows * cols, width), jnp.bfloat16),
        in_specs=[VMEM],
        out_specs=VMEM,
        compiler_params=ROOM,
        cost_estimate=pl.CostEstimate(
            flops=8 * rows * cols * width * width, bytes_accessed=4 * 1024 * 1024, transcendentals=0
        ),
    )(pair)


def project_kernel(normed_ref, valid_ref, w_ref, sent_ref, held):
    hidden, both, cols = sent_ref.shape
    rows = both // 2
    turned = w_ref[...].T
    valid = valid_ref[...].astype(jnp.float32)
    seat = lax.broadcasted_iota(jnp.int32, valid.shape, 1)
    first = lax.axis_index("wide") * rows
    col_valid = jnp.where(lax.axis_index("row") == 0, valid[:, :cols], valid[:, cols:])
    for row in range(rows):
        row_valid = jnp.sum(jnp.where(seat == first + row, valid, 0.0), axis=1, keepdims=True)
        mask = row_valid * col_valid
        proj = dot_rows(turned, normed_ref[pl.ds(row * cols, cols), :])
        left = sigmoid(proj[:hidden]) * proj[hidden : 2 * hidden] * mask
        right = sigmoid(proj[2 * hidden : 3 * hidden]) * proj[3 * hidden :] * mask
        held[row] = left.astype(jnp.bfloat16)
        held[rows + row] = right.astype(jnp.bfloat16)
    step = 16
    for first_channel in range(0, hidden, step):
        part = slice(first_channel, first_channel + step)
        sent_ref[part] = jnp.transpose(held[:, part, :], (1, 0, 2))


def project_blocks(normed, token_valid, w_pair, rows, hidden):
    cols = normed.shape[0] // rows
    return pl.pallas_call(
        project_kernel,
        out_shape=jax.ShapeDtypeStruct((hidden, 2 * rows, cols), jnp.bfloat16),
        in_specs=[VMEM] * 3,
        out_specs=VMEM,
        scratch_shapes=[pltpu.VMEM((2 * rows, hidden, cols), jnp.bfloat16)],
        compiler_params=ROOM,
    )(normed, token_valid.reshape(1, -1), w_pair)


def flat(values):
    chips, rows, cols = values.shape
    return values.astype(jnp.float32).reshape(chips * rows, cols).astype(jnp.bfloat16)


def own_kernel(
    seats, got_ref, normed_ref, gate_ref, w_out_ref, left_ref, own_ref, gating_ref, held_out_ref
):
    held_out_ref[...] = w_out_ref[...]
    blocks, both, cols = got_ref.shape
    rows, chips = both // 2, blocks // 2
    for half in range(2):
        part = seats[half * chips : (half + 1) * chips]
        got = jnp.stack([got_ref[seat] for seat in part])
        left_ref[half] = flat(got[:, :rows, :])
        own_ref[half] = got[:, rows:, :].astype(jnp.float32)
    gating_ref[...] = sigmoid(
        jnp.dot(normed_ref[...], gate_ref[...], preferred_element_type=jnp.float32)
    )


def own_part(seats, got, normed, w_gate, w_out):
    blocks, both, cols = got.shape
    rows, chips = both // 2, blocks // 2
    return pl.pallas_call(
        functools.partial(own_kernel, seats),
        out_shape=(
            jax.ShapeDtypeStruct((2, chips * rows, cols), jnp.bfloat16),
            jax.ShapeDtypeStruct((2, chips, rows, cols), jnp.float32),
            jax.ShapeDtypeStruct(normed.shape, jnp.float32),
            jax.ShapeDtypeStruct(w_out.shape, jnp.bfloat16),
        ),
        in_specs=[VMEM] * 4,
        out_specs=(VMEM,) * 4,
        compiler_params=ROOM,
        cost_estimate=pl.CostEstimate(
            flops=4 * (chips * rows) ** 2 * cols, bytes_accessed=3 * 1024 * 1024, transcendentals=0
        ),
    )(got, normed, w_gate, w_out)


def plane_kernel(seats, other_ref, left_ref, own_ref, out_ref):
    blocks, rows, cols = other_ref.shape
    chips = blocks // 2
    plane = jnp.zeros((chips * rows, 2 * chips * rows), jnp.float32)
    first = lax.axis_index("wide") % 2 == 0
    for half in range(2):
        part = seats[half * chips : (half + 1) * chips]
        own = own_ref[half]
        other = jnp.stack([other_ref[seat] for seat in part]).astype(jnp.float32)
        right = jnp.concatenate(
            [jnp.where(first, own, other), jnp.where(first, other, own)], axis=1
        )
        plane += dot_rows(left_ref[half], right.reshape(-1, cols).astype(jnp.bfloat16))
    for half in range(2):
        placed = plane[:, half * cols : (half + 1) * cols].reshape(chips, rows, cols)
        tiles = jnp.concatenate([placed[:, :, : cols // 2], placed[:, :, cols // 2 :]], axis=1)
        tiles = tiles.astype(jnp.bfloat16)
        for chip in range(chips):
            out_ref[seats[half * chips + chip]] = tiles[chip]


def plane_blocks(seats, other, left, own):
    blocks, rows, cols = other.shape
    return pl.pallas_call(
        functools.partial(plane_kernel, seats),
        out_shape=jax.ShapeDtypeStruct((blocks, 2 * rows, cols // 2), jnp.bfloat16),
        in_specs=[VMEM] * 3,
        out_specs=VMEM,
        compiler_params=ROOM,
    )(other, left, own)


def finish_kernel(returned_ref, gating_ref, out_ref, update_hbm, staged, left_device):
    rows, cols, width = staged.shape
    hidden = returned_ref.shape[0]
    turned = jnp.transpose(returned_ref[...], (1, 0, 2))
    copies = []
    for row in range(rows):
        values = jnp.concatenate([turned[row], turned[rows + row]], axis=1).astype(jnp.float32)
        mean = jnp.sum(values, axis=0, keepdims=True) * (1.0 / hidden)
        centered = values - mean
        spread = jnp.sum(centered * centered, axis=0, keepdims=True) * (1.0 / hidden)
        tri_norm = (centered * lax.rsqrt(spread + 1e-05)).astype(jnp.bfloat16)
        mixed = lax.dot_general(
            tri_norm, out_ref[...], (((0,), (0,)), ((), ())), preferred_element_type=jnp.float32
        )
        staged[row] = (gating_ref[pl.ds(row * cols, cols), :] * mixed).astype(jnp.bfloat16)
        copy = pltpu.make_async_copy(staged.at[row], update_hbm.at[row], left_device.at[row])
        copy.start()
        copies.append(copy)
    for copy in copies:
        copy.wait()


def finish(returned, gating, w_out, shape):
    return pl.pallas_call(
        finish_kernel,
        out_shape=jax.ShapeDtypeStruct(shape, jnp.bfloat16),
        in_specs=[VMEM] * 3,
        out_specs=ANY,
        scratch_shapes=[
            pltpu.VMEM(shape, jnp.bfloat16),
            pltpu.SemaphoreType.DMA((shape[0],)),
        ],
        compiler_params=ROOM,
    )(returned, gating, w_out)


def make(wide, row):
    order = group_order(wide // 2, row)
    groups = chip_groups(order, row)
    seats = [order.index(number) for number in range(len(order))]

    def shards(pair, token_valid, w_pair, w_gate, w_out):
        rows = pair.shape[0]
        normed = norm_pair(pair)
        sent = project_blocks(normed, token_valid, w_pair, rows, w_out.shape[0])
        got = exchange(sent, groups)
        other = lax.ppermute(got[:, rows:, :], "wide", [(i, i ^ 1) for i in range(wide)])
        left, own, gating, w_out = own_part(seats, got, normed, w_gate, w_out)
        returned = exchange(plane_blocks(seats, other, left, own), groups)
        return finish(returned, gating, w_out, pair.shape)

    return shards


def solution(mesh):
    placed = (P("wide", "row", None), P(), P(), P(), P())
    return jax.shard_map(
        make(mesh.shape["wide"], mesh.shape["row"]),
        mesh=mesh,
        in_specs=placed,
        out_specs=P("wide", "row", None),
        check_vma=False,
    )
```

```python
import functools

import jax
import jax.numpy as jnp
from jax import lax
from jax.experimental import pallas as pl
from jax.experimental.pallas import tpu as pltpu
from jax.sharding import PartitionSpec as P

VMEM = pl.BlockSpec(memory_space=pltpu.VMEM)
ANY = pl.BlockSpec(memory_space=pl.ANY)
HBM = pl.BlockSpec(memory_space=pltpu.HBM)
ROOM = pltpu.CompilerParams(vmem_limit_bytes=32 * 1024 * 1024)


Y, Z, X = 4, 8, 4
LEAD = (2, 5, 2)


def group_order(chips, row):
    def place(number):
        half, chip = divmod(number, chips)
        x_in = X // row
        return chip // (x_in * Z), chip // x_in % Z, half * x_in + chip % x_in

    def apart(number):
        y, z, x = place(number)
        along = abs(z - LEAD[1])
        return abs(y - LEAD[0]) + min(along, Z - along) + abs(x - LEAD[2])

    return sorted(range(row * chips), key=lambda number: (apart(number) > 0, -apart(number)))


def chip_groups(order, row):
    chips = len(order) // row
    return [
        [(number % chips * 2 + core) * row + number // chips for number in order]
        for core in range(2)
    ]


def exchange(blocks, groups):
    return lax.all_to_all(
        blocks, ("wide", "row"), split_axis=0, concat_axis=0, tiled=True, axis_index_groups=groups
    )


def dot_rows(left, right):
    return lax.dot_general(
        left, right, (((1,), (1,)), ((), ())), preferred_element_type=jnp.float32
    )


def sigmoid(values):
    return 0.5 * jnp.tanh(0.5 * values) + 0.5


def weights_kernel(w_hbm, valid_hbm, share_ref, turned_ref, valid_ref, w_ref, arrived):
    part = w_ref.shape[0] // 4
    pieces = [
        (w_hbm.at[pl.ds(at * part, part)], w_ref.at[pl.ds(at * part, part)]) for at in range(4)
    ]
    pieces += [(valid_hbm, valid_ref)]
    copies = [
        pltpu.make_async_copy(source, target, arrived.at[index])
        for index, (source, target) in enumerate(pieces)
    ]
    for copy in copies:
        copy.start()
    share_ref[...] = jnp.full(share_ref.shape, 1.0 / share_ref.shape[1], jnp.bfloat16)
    for copy in copies:
        copy.wait()
    turned_ref[...] = w_ref[...].T


def prepare_weights(w_pair, valid):
    width, outs = w_pair.shape
    return pl.pallas_call(
        weights_kernel,
        out_shape=(
            jax.ShapeDtypeStruct((2 * width, width), jnp.bfloat16),
            jax.ShapeDtypeStruct((outs, width), jnp.bfloat16),
            jax.ShapeDtypeStruct(valid.shape, jnp.int32),
        ),
        in_specs=[HBM] * 2,
        out_specs=(VMEM,) * 3,
        scratch_shapes=[
            pltpu.VMEM(w_pair.shape, jnp.bfloat16),
            pltpu.SemaphoreType.DMA((5,)),
        ],
        compiler_params=ROOM,
        cost_estimate=pl.CostEstimate(
            flops=1024**3, bytes_accessed=8 * 1024 * 1024, transcendentals=0
        ),
    )(*(pltpu.with_memory_space_constraint(value, pltpu.HBM) for value in (w_pair, valid)))


def normed_kernel(pair_ref, share_ref, normed_ref):
    rows, cols, width = pair_ref.shape

    def mean(values):
        return jnp.dot(
            values, share_ref[: values.shape[1], :], preferred_element_type=jnp.float32
        )

    step = rows // 2
    for first in range(0, rows, step):
        values = pair_ref[pl.ds(first, step)].reshape(step * cols, width)
        centered = values.astype(jnp.float32) - mean(values)
        square = centered * centered
        high = square.astype(jnp.bfloat16)
        low = (square - high.astype(jnp.float32)).astype(jnp.bfloat16)
        spread = mean(jnp.concatenate([high, low], axis=1))
        normed_ref[pl.ds(first * cols, step * cols), :] = (
            centered * lax.rsqrt(spread + 1e-05)
        ).astype(jnp.bfloat16)


def norm_pair(pair, share):
    rows, cols, width = pair.shape
    return pl.pallas_call(
        normed_kernel,
        out_shape=jax.ShapeDtypeStruct((rows * cols, width), jnp.bfloat16),
        in_specs=[VMEM] * 2,
        out_specs=VMEM,
        compiler_params=ROOM,
        cost_estimate=pl.CostEstimate(
            flops=8 * rows * cols * width * width, bytes_accessed=4 * 1024 * 1024, transcendentals=0
        ),
    )(pair, share)


def project_kernel(normed_ref, valid_ref, turned_ref, sent_ref, held):
    hidden, both, cols = sent_ref.shape
    rows = both // 2
    valid = valid_ref[...].astype(jnp.float32)
    seat = lax.broadcasted_iota(jnp.int32, valid.shape, 1)
    first = lax.axis_index("wide") * rows
    col_valid = jnp.where(lax.axis_index("row") == 0, valid[:, :cols], valid[:, cols:])
    for row in range(rows):
        row_valid = jnp.sum(jnp.where(seat == first + row, valid, 0.0), axis=1, keepdims=True)
        mask = row_valid * col_valid
        proj = dot_rows(turned_ref[...], normed_ref[pl.ds(row * cols, cols), :])
        left = sigmoid(proj[:hidden]) * proj[hidden : 2 * hidden] * mask
        right = sigmoid(proj[2 * hidden : 3 * hidden]) * proj[3 * hidden :] * mask
        held[row] = left.astype(jnp.bfloat16)
        held[rows + row] = right.astype(jnp.bfloat16)
    step = 16
    for first_channel in range(0, hidden, step):
        part = slice(first_channel, first_channel + step)
        sent_ref[part] = jnp.transpose(held[:, part, :], (1, 0, 2))


def project_blocks(normed, valid, turned, rows, hidden):
    cols = normed.shape[0] // rows
    return pl.pallas_call(
        project_kernel,
        out_shape=jax.ShapeDtypeStruct((hidden, 2 * rows, cols), jnp.bfloat16),
        in_specs=[VMEM] * 3,
        out_specs=VMEM,
        scratch_shapes=[pltpu.VMEM((2 * rows, hidden, cols), jnp.bfloat16)],
        compiler_params=ROOM,
    )(normed, valid, turned)


def flat(values):
    chips, rows, cols = values.shape
    return values.astype(jnp.float32).reshape(chips * rows, cols).astype(jnp.bfloat16)


def own_kernel(
    seats, got_ref, normed_ref, gate_ref, w_out_ref, left_ref, own_ref, gating_ref, held_out_ref
):
    held_out_ref[...] = w_out_ref[...]
    blocks, both, cols = got_ref.shape
    rows, chips = both // 2, blocks // 2
    for half in range(2):
        part = seats[half * chips : (half + 1) * chips]
        got = jnp.stack([got_ref[seat] for seat in part])
        left_ref[half] = flat(got[:, :rows, :])
        own_ref[half] = got[:, rows:, :].astype(jnp.float32)
    gating_ref[...] = sigmoid(
        jnp.dot(normed_ref[...], gate_ref[...], preferred_element_type=jnp.float32)
    )


def own_part(seats, got, normed, w_gate, w_out):
    blocks, both, cols = got.shape
    rows, chips = both // 2, blocks // 2
    return pl.pallas_call(
        functools.partial(own_kernel, seats),
        out_shape=(
            jax.ShapeDtypeStruct((2, chips * rows, cols), jnp.bfloat16),
            jax.ShapeDtypeStruct((2, chips, rows, cols), jnp.float32),
            jax.ShapeDtypeStruct(normed.shape, jnp.float32),
            jax.ShapeDtypeStruct(w_out.shape, jnp.bfloat16),
        ),
        in_specs=[VMEM] * 4,
        out_specs=(VMEM,) * 4,
        compiler_params=ROOM,
        cost_estimate=pl.CostEstimate(
            flops=4 * (chips * rows) ** 2 * cols, bytes_accessed=3 * 1024 * 1024, transcendentals=0
        ),
    )(got, normed, w_gate, w_out)


def plane_kernel(seats, other_ref, left_ref, own_ref, out_ref):
    blocks, rows, cols = other_ref.shape
    chips = blocks // 2
    plane = jnp.zeros((chips * rows, 2 * chips * rows), jnp.float32)
    first = lax.axis_index("wide") % 2 == 0
    for half in range(2):
        part = seats[half * chips : (half + 1) * chips]
        own = own_ref[half]
        other = jnp.stack([other_ref[seat] for seat in part]).astype(jnp.float32)
        right = jnp.concatenate(
            [jnp.where(first, own, other), jnp.where(first, other, own)], axis=1
        )
        plane += dot_rows(left_ref[half], right.reshape(-1, cols).astype(jnp.bfloat16))
    for half in range(2):
        placed = plane[:, half * cols : (half + 1) * cols].reshape(chips, rows, cols)
        tiles = jnp.concatenate([placed[:, :, : cols // 2], placed[:, :, cols // 2 :]], axis=1)
        tiles = tiles.astype(jnp.bfloat16)
        for chip in range(chips):
            out_ref[seats[half * chips + chip]] = tiles[chip]


def plane_blocks(seats, other, left, own):
    blocks, rows, cols = other.shape
    return pl.pallas_call(
        functools.partial(plane_kernel, seats),
        out_shape=jax.ShapeDtypeStruct((blocks, 2 * rows, cols // 2), jnp.bfloat16),
        in_specs=[VMEM] * 3,
        out_specs=VMEM,
        compiler_params=ROOM,
    )(other, left, own)


def finish_kernel(returned_ref, gating_ref, out_ref, update_hbm, staged, left_device):
    rows, cols, width = staged.shape
    hidden = returned_ref.shape[0]
    turned = jnp.transpose(returned_ref[...], (1, 0, 2))
    copies = []
    for row in range(rows):
        values = jnp.concatenate([turned[row], turned[rows + row]], axis=1).astype(jnp.float32)
        mean = jnp.sum(values, axis=0, keepdims=True) * (1.0 / hidden)
        centered = values - mean
        spread = jnp.sum(centered * centered, axis=0, keepdims=True) * (1.0 / hidden)
        tri_norm = (centered * lax.rsqrt(spread + 1e-05)).astype(jnp.bfloat16)
        mixed = lax.dot_general(
            tri_norm, out_ref[...], (((0,), (0,)), ((), ())), preferred_element_type=jnp.float32
        )
        staged[row] = (gating_ref[pl.ds(row * cols, cols), :] * mixed).astype(jnp.bfloat16)
        copy = pltpu.make_async_copy(staged.at[row], update_hbm.at[row], left_device.at[row])
        copy.start()
        copies.append(copy)
    for copy in copies:
        copy.wait()


def finish(returned, gating, w_out, shape):
    return pl.pallas_call(
        finish_kernel,
        out_shape=jax.ShapeDtypeStruct(shape, jnp.bfloat16),
        in_specs=[VMEM] * 3,
        out_specs=ANY,
        scratch_shapes=[
            pltpu.VMEM(shape, jnp.bfloat16),
            pltpu.SemaphoreType.DMA((shape[0],)),
        ],
        compiler_params=ROOM,
    )(returned, gating, w_out)


def make(wide, row):
    order = group_order(wide // 2, row)
    groups = chip_groups(order, row)
    seats = [order.index(number) for number in range(len(order))]

    def shards(pair, token_valid, w_pair, w_gate, w_out):
        rows = pair.shape[0]
        share, turned, valid = prepare_weights(w_pair, token_valid.reshape(1, -1))
        normed = norm_pair(pair, share)
        sent = project_blocks(normed, valid, turned, rows, w_out.shape[0])
        got = exchange(sent, groups)
        other = lax.ppermute(got[:, rows:, :], "wide", [(i, i ^ 1) for i in range(wide)])
        left, own, gating, w_out = own_part(seats, got, normed, w_gate, w_out)
        returned = exchange(plane_blocks(seats, other, left, own), groups)
        return finish(returned, gating, w_out, pair.shape)

    return shards


def solution(mesh):
    placed = (P("wide", "row", None), P(), P(), P(), P())
    return jax.shard_map(
        make(mesh.shape["wide"], mesh.shape["row"]),
        mesh=mesh,
        in_specs=placed,
        out_specs=P("wide", "row", None),
        check_vma=False,
    )
```

```python
import functools

import jax
import jax.numpy as jnp
from jax import lax
from jax.experimental import pallas as pl
from jax.experimental.pallas import tpu as pltpu
from jax.sharding import PartitionSpec as P

VMEM = pl.BlockSpec(memory_space=pltpu.VMEM)
ANY = pl.BlockSpec(memory_space=pl.ANY)
HBM = pl.BlockSpec(memory_space=pltpu.HBM)
ROOM = pltpu.CompilerParams(vmem_limit_bytes=32 * 1024 * 1024)


Y, Z, X = 4, 8, 4
LEAD = (2, 5, 2)


def group_order(chips, row):
    def place(number):
        half, chip = divmod(number, chips)
        x_in = X // row
        return chip // (x_in * Z), chip // x_in % Z, half * x_in + chip % x_in

    def apart(number):
        y, z, x = place(number)
        along = abs(z - LEAD[1])
        return abs(y - LEAD[0]) + min(along, Z - along) + abs(x - LEAD[2])

    return sorted(range(row * chips), key=lambda number: (apart(number) > 0, -apart(number)))


def chip_groups(order, row):
    chips = len(order) // row
    return [
        [(number % chips * 2 + core) * row + number // chips for number in order]
        for core in range(2)
    ]


def exchange(blocks, groups):
    return lax.all_to_all(
        blocks, ("wide", "row"), split_axis=0, concat_axis=0, tiled=True, axis_index_groups=groups
    )


def dot_rows(left, right):
    return lax.dot_general(
        left, right, (((1,), (1,)), ((), ())), preferred_element_type=jnp.float32
    )


def sigmoid(values):
    return 1.0 / (1.0 + jnp.exp(-values))


def weights_kernel(w_hbm, valid_hbm, share_ref, turned_ref, valid_ref, w_ref, arrived):
    part = w_ref.shape[0] // 4
    pieces = [
        (w_hbm.at[pl.ds(at * part, part)], w_ref.at[pl.ds(at * part, part)]) for at in range(4)
    ]
    pieces += [(valid_hbm, valid_ref)]
    copies = [
        pltpu.make_async_copy(source, target, arrived.at[index])
        for index, (source, target) in enumerate(pieces)
    ]
    for copy in copies:
        copy.start()
    share_ref[...] = jnp.full(share_ref.shape, 1.0 / share_ref.shape[1], jnp.bfloat16)
    for copy in copies:
        copy.wait()
    turned_ref[...] = w_ref[...].T


def prepare_weights(w_pair, valid):
    width, outs = w_pair.shape
    return pl.pallas_call(
        weights_kernel,
        out_shape=(
            jax.ShapeDtypeStruct((2 * width, width), jnp.bfloat16),
            jax.ShapeDtypeStruct((outs, width), jnp.bfloat16),
            jax.ShapeDtypeStruct(valid.shape, jnp.int32),
        ),
        in_specs=[HBM] * 2,
        out_specs=(VMEM,) * 3,
        scratch_shapes=[
            pltpu.VMEM(w_pair.shape, jnp.bfloat16),
            pltpu.SemaphoreType.DMA((5,)),
        ],
        compiler_params=ROOM,
        cost_estimate=pl.CostEstimate(
            flops=1024**3, bytes_accessed=8 * 1024 * 1024, transcendentals=0
        ),
    )(*(pltpu.with_memory_space_constraint(value, pltpu.HBM) for value in (w_pair, valid)))


def normed_kernel(pair_ref, share_ref, normed_ref):
    rows, cols, width = pair_ref.shape

    def mean(values):
        return jnp.dot(
            values, share_ref[: values.shape[1], :], preferred_element_type=jnp.float32
        )

    step = rows // 2
    for first in range(0, rows, step):
        values = pair_ref[pl.ds(first, step)].reshape(step * cols, width)
        centered = values.astype(jnp.float32) - mean(values)
        square = centered * centered
        high = square.astype(jnp.bfloat16)
        low = (square - high.astype(jnp.float32)).astype(jnp.bfloat16)
        spread = mean(jnp.concatenate([high, low], axis=1))
        normed_ref[pl.ds(first * cols, step * cols), :] = (
            centered * lax.rsqrt(spread + 1e-05)
        ).astype(jnp.bfloat16)


def norm_pair(pair, share):
    rows, cols, width = pair.shape
    return pl.pallas_call(
        normed_kernel,
        out_shape=jax.ShapeDtypeStruct((rows * cols, width), jnp.bfloat16),
        in_specs=[VMEM] * 2,
        out_specs=VMEM,
        compiler_params=ROOM,
        cost_estimate=pl.CostEstimate(
            flops=8 * rows * cols * width * width, bytes_accessed=4 * 1024 * 1024, transcendentals=0
        ),
    )(pair, share)


def project_kernel(normed_ref, valid_ref, turned_ref, sent_ref, held):
    hidden, both, cols = sent_ref.shape
    rows = both // 2
    valid = valid_ref[...].astype(jnp.float32)
    seat = lax.broadcasted_iota(jnp.int32, valid.shape, 1)
    first = lax.axis_index("wide") * rows
    col_valid = jnp.where(lax.axis_index("row") == 0, valid[:, :cols], valid[:, cols:])
    for row in range(rows):
        row_valid = jnp.sum(jnp.where(seat == first + row, valid, 0.0), axis=1, keepdims=True)
        mask = row_valid * col_valid
        proj = dot_rows(turned_ref[...], normed_ref[pl.ds(row * cols, cols), :])
        left = sigmoid(proj[:hidden]) * proj[hidden : 2 * hidden] * mask
        right = sigmoid(proj[2 * hidden : 3 * hidden]) * proj[3 * hidden :] * mask
        held[row] = left.astype(jnp.bfloat16)
        held[rows + row] = right.astype(jnp.bfloat16)
    step = 16
    for first_channel in range(0, hidden, step):
        part = slice(first_channel, first_channel + step)
        sent_ref[part] = jnp.transpose(held[:, part, :], (1, 0, 2))


def project_blocks(normed, valid, turned, rows, hidden):
    cols = normed.shape[0] // rows
    return pl.pallas_call(
        project_kernel,
        out_shape=jax.ShapeDtypeStruct((hidden, 2 * rows, cols), jnp.bfloat16),
        in_specs=[VMEM] * 3,
        out_specs=VMEM,
        scratch_shapes=[pltpu.VMEM((2 * rows, hidden, cols), jnp.bfloat16)],
        compiler_params=ROOM,
    )(normed, valid, turned)


def flat(values):
    chips, rows, cols = values.shape
    return values.astype(jnp.float32).reshape(chips * rows, cols).astype(jnp.bfloat16)


def own_kernel(
    seats, got_ref, normed_ref, gate_ref, w_out_ref, left_ref, own_ref, gating_ref, held_out_ref
):
    held_out_ref[...] = w_out_ref[...]
    blocks, both, cols = got_ref.shape
    rows, chips = both // 2, blocks // 2
    for half in range(2):
        part = seats[half * chips : (half + 1) * chips]
        got = jnp.stack([got_ref[seat] for seat in part])
        left_ref[half] = flat(got[:, :rows, :])
        own_ref[half] = got[:, rows:, :].astype(jnp.float32)
    gating_ref[...] = sigmoid(
        jnp.dot(normed_ref[...], gate_ref[...], preferred_element_type=jnp.float32)
    )


def own_part(seats, got, normed, w_gate, w_out):
    blocks, both, cols = got.shape
    rows, chips = both // 2, blocks // 2
    return pl.pallas_call(
        functools.partial(own_kernel, seats),
        out_shape=(
            jax.ShapeDtypeStruct((2, chips * rows, cols), jnp.bfloat16),
            jax.ShapeDtypeStruct((2, chips, rows, cols), jnp.float32),
            jax.ShapeDtypeStruct(normed.shape, jnp.float32),
            jax.ShapeDtypeStruct(w_out.shape, jnp.bfloat16),
        ),
        in_specs=[VMEM] * 4,
        out_specs=(VMEM,) * 4,
        compiler_params=ROOM,
        cost_estimate=pl.CostEstimate(
            flops=4 * (chips * rows) ** 2 * cols, bytes_accessed=3 * 1024 * 1024, transcendentals=0
        ),
    )(got, normed, w_gate, w_out)


def plane_kernel(seats, other_ref, left_ref, own_ref, out_ref):
    blocks, rows, cols = other_ref.shape
    chips = blocks // 2
    plane = jnp.zeros((chips * rows, 2 * chips * rows), jnp.float32)
    first = lax.axis_index("wide") % 2 == 0
    for half in range(2):
        part = seats[half * chips : (half + 1) * chips]
        own = own_ref[half]
        other = jnp.stack([other_ref[seat] for seat in part]).astype(jnp.float32)
        right = jnp.concatenate(
            [jnp.where(first, own, other), jnp.where(first, other, own)], axis=1
        )
        plane += dot_rows(left_ref[half], right.reshape(-1, cols).astype(jnp.bfloat16))
    for half in range(2):
        placed = plane[:, half * cols : (half + 1) * cols].reshape(chips, rows, cols)
        tiles = jnp.concatenate([placed[:, :, : cols // 2], placed[:, :, cols // 2 :]], axis=1)
        tiles = tiles.astype(jnp.bfloat16)
        for chip in range(chips):
            out_ref[seats[half * chips + chip]] = tiles[chip]


def plane_blocks(seats, other, left, own):
    blocks, rows, cols = other.shape
    return pl.pallas_call(
        functools.partial(plane_kernel, seats),
        out_shape=jax.ShapeDtypeStruct((blocks, 2 * rows, cols // 2), jnp.bfloat16),
        in_specs=[VMEM] * 3,
        out_specs=VMEM,
        compiler_params=ROOM,
    )(other, left, own)


def finish_kernel(returned_ref, gating_ref, out_ref, update_hbm, staged, left_device):
    rows, cols, width = staged.shape
    hidden = returned_ref.shape[0]
    turned = jnp.transpose(returned_ref[...], (1, 0, 2))
    copies = []
    for row in range(rows):
        values = jnp.concatenate([turned[row], turned[rows + row]], axis=1).astype(jnp.float32)
        mean = jnp.sum(values, axis=0, keepdims=True) * (1.0 / hidden)
        centered = values - mean
        spread = jnp.sum(centered * centered, axis=0, keepdims=True) * (1.0 / hidden)
        tri_norm = (centered * lax.rsqrt(spread + 1e-05)).astype(jnp.bfloat16)
        mixed = lax.dot_general(
            tri_norm, out_ref[...], (((0,), (0,)), ((), ())), preferred_element_type=jnp.float32
        )
        staged[row] = (gating_ref[pl.ds(row * cols, cols), :] * mixed).astype(jnp.bfloat16)
        copy = pltpu.make_async_copy(staged.at[row], update_hbm.at[row], left_device.at[row])
        copy.start()
        copies.append(copy)
    for copy in copies:
        copy.wait()


def finish(returned, gating, w_out, shape):
    return pl.pallas_call(
        finish_kernel,
        out_shape=jax.ShapeDtypeStruct(shape, jnp.bfloat16),
        in_specs=[VMEM] * 3,
        out_specs=ANY,
        scratch_shapes=[
            pltpu.VMEM(shape, jnp.bfloat16),
            pltpu.SemaphoreType.DMA((shape[0],)),
        ],
        compiler_params=ROOM,
    )(returned, gating, w_out)


def make(wide, row):
    order = group_order(wide // 2, row)
    groups = chip_groups(order, row)
    seats = [order.index(number) for number in range(len(order))]

    def shards(pair, token_valid, w_pair, w_gate, w_out):
        rows = pair.shape[0]
        share, turned, valid = prepare_weights(w_pair, token_valid.reshape(1, -1))
        normed = norm_pair(pair, share)
        sent = project_blocks(normed, valid, turned, rows, w_out.shape[0])
        got = exchange(sent, groups)
        other = lax.ppermute(got[:, rows:, :], "wide", [(i, i ^ 1) for i in range(wide)])
        left, own, gating, w_out = own_part(seats, got, normed, w_gate, w_out)
        returned = exchange(plane_blocks(seats, other, left, own), groups)
        return finish(returned, gating, w_out, pair.shape)

    return shards


def solution(mesh):
    placed = (P("wide", "row", None), P(), P(), P(), P())
    return jax.shard_map(
        make(mesh.shape["wide"], mesh.shape["row"]),
        mesh=mesh,
        in_specs=placed,
        out_specs=P("wide", "row", None),
        check_vma=False,
    )
```

```python
import functools

import jax
import jax.numpy as jnp
from jax import lax
from jax.experimental import pallas as pl
from jax.experimental.pallas import tpu as pltpu
from jax.sharding import PartitionSpec as P

VMEM = pl.BlockSpec(memory_space=pltpu.VMEM)
ANY = pl.BlockSpec(memory_space=pl.ANY)
HBM = pl.BlockSpec(memory_space=pltpu.HBM)
ROOM = pltpu.CompilerParams(vmem_limit_bytes=32 * 1024 * 1024)


Y, Z, X = 4, 8, 4
LEAD = (2, 5, 2)


def group_order(chips, row):
    def place(number):
        half, chip = divmod(number, chips)
        x_in = X // row
        return chip // (x_in * Z), chip // x_in % Z, half * x_in + chip % x_in

    def apart(number):
        y, z, x = place(number)
        along = abs(z - LEAD[1])
        return abs(y - LEAD[0]) + min(along, Z - along) + abs(x - LEAD[2])

    return sorted(range(row * chips), key=lambda number: (apart(number) > 0, -apart(number)))


def chip_groups(order, row):
    chips = len(order) // row
    return [
        [(number % chips * 2 + core) * row + number // chips for number in order]
        for core in range(2)
    ]


def exchange(blocks, groups):
    return lax.all_to_all(
        blocks, ("wide", "row"), split_axis=0, concat_axis=0, tiled=True, axis_index_groups=groups
    )


def dot_rows(left, right):
    return lax.dot_general(
        left, right, (((1,), (1,)), ((), ())), preferred_element_type=jnp.float32
    )


def sigmoid(values):
    return 1.0 / (1.0 + jnp.exp(-values))


def weights_kernel(
    w_hbm, valid_hbm, gate_hbm, out_hbm,
    share_ref, turned_ref, valid_ref, gate_ref, out_ref, w_ref, arrived,
):
    part = w_ref.shape[0] // 4
    pieces = [
        (w_hbm.at[pl.ds(at * part, part)], w_ref.at[pl.ds(at * part, part)]) for at in range(4)
    ]
    pieces += [(valid_hbm, valid_ref), (gate_hbm, gate_ref), (out_hbm, out_ref)]
    copies = [
        pltpu.make_async_copy(source, target, arrived.at[index])
        for index, (source, target) in enumerate(pieces)
    ]
    for copy in copies:
        copy.start()
    share_ref[...] = jnp.full(share_ref.shape, 1.0 / share_ref.shape[1], jnp.bfloat16)
    for copy in copies[:4]:
        copy.wait()
    turned_ref[...] = w_ref[...].T
    for copy in copies[4:]:
        copy.wait()


def prepare_weights(w_pair, valid, w_gate, w_out):
    width, outs = w_pair.shape
    return pl.pallas_call(
        weights_kernel,
        out_shape=(
            jax.ShapeDtypeStruct((2 * width, width), jnp.bfloat16),
            jax.ShapeDtypeStruct((outs, width), jnp.bfloat16),
            jax.ShapeDtypeStruct(valid.shape, jnp.int32),
            jax.ShapeDtypeStruct(w_gate.shape, jnp.bfloat16),
            jax.ShapeDtypeStruct(w_out.shape, jnp.bfloat16),
        ),
        in_specs=[HBM] * 4,
        out_specs=(VMEM,) * 5,
        scratch_shapes=[
            pltpu.VMEM(w_pair.shape, jnp.bfloat16),
            pltpu.SemaphoreType.DMA((7,)),
        ],
        compiler_params=ROOM,
        cost_estimate=pl.CostEstimate(
            flops=1024**3, bytes_accessed=8 * 1024 * 1024, transcendentals=0
        ),
    )(
        *(
            pltpu.with_memory_space_constraint(value, pltpu.HBM)
            for value in (w_pair, valid, w_gate, w_out)
        )
    )


def normed_kernel(pair_ref, share_ref, normed_ref):
    rows, cols, width = pair_ref.shape

    def mean(values):
        return jnp.dot(
            values, share_ref[: values.shape[1], :], preferred_element_type=jnp.float32
        )

    step = rows // 2
    for first in range(0, rows, step):
        values = pair_ref[pl.ds(first, step)].reshape(step * cols, width)
        centered = values.astype(jnp.float32) - mean(values)
        square = centered * centered
        high = square.astype(jnp.bfloat16)
        low = (square - high.astype(jnp.float32)).astype(jnp.bfloat16)
        spread = mean(jnp.concatenate([high, low], axis=1))
        normed_ref[pl.ds(first * cols, step * cols), :] = (
            centered * lax.rsqrt(spread + 1e-05)
        ).astype(jnp.bfloat16)


def norm_pair(pair, share):
    rows, cols, width = pair.shape
    return pl.pallas_call(
        normed_kernel,
        out_shape=jax.ShapeDtypeStruct((rows * cols, width), jnp.bfloat16),
        in_specs=[VMEM] * 2,
        out_specs=VMEM,
        compiler_params=ROOM,
        cost_estimate=pl.CostEstimate(
            flops=8 * rows * cols * width * width, bytes_accessed=4 * 1024 * 1024, transcendentals=0
        ),
    )(pair, share)


def project_kernel(normed_ref, valid_ref, turned_ref, sent_ref, held):
    hidden, both, cols = sent_ref.shape
    rows = both // 2
    valid = valid_ref[...].astype(jnp.float32)
    seat = lax.broadcasted_iota(jnp.int32, valid.shape, 1)
    first = lax.axis_index("wide") * rows
    col_valid = jnp.where(lax.axis_index("row") == 0, valid[:, :cols], valid[:, cols:])
    for row in range(rows):
        row_valid = jnp.sum(jnp.where(seat == first + row, valid, 0.0), axis=1, keepdims=True)
        mask = row_valid * col_valid
        proj = dot_rows(turned_ref[...], normed_ref[pl.ds(row * cols, cols), :])
        left = sigmoid(proj[:hidden]) * proj[hidden : 2 * hidden] * mask
        right = sigmoid(proj[2 * hidden : 3 * hidden]) * proj[3 * hidden :] * mask
        held[row] = left.astype(jnp.bfloat16)
        held[rows + row] = right.astype(jnp.bfloat16)
    step = 16
    for first_channel in range(0, hidden, step):
        part = slice(first_channel, first_channel + step)
        sent_ref[part] = jnp.transpose(held[:, part, :], (1, 0, 2))


def project_blocks(normed, valid, turned, rows, hidden):
    cols = normed.shape[0] // rows
    return pl.pallas_call(
        project_kernel,
        out_shape=jax.ShapeDtypeStruct((hidden, 2 * rows, cols), jnp.bfloat16),
        in_specs=[VMEM] * 3,
        out_specs=VMEM,
        scratch_shapes=[pltpu.VMEM((2 * rows, hidden, cols), jnp.bfloat16)],
        compiler_params=ROOM,
    )(normed, valid, turned)


def flat(values):
    chips, rows, cols = values.shape
    return values.astype(jnp.float32).reshape(chips * rows, cols).astype(jnp.bfloat16)


def own_kernel(seats, got_ref, normed_ref, gate_ref, left_ref, own_ref, gating_ref):
    blocks, both, cols = got_ref.shape
    rows, chips = both // 2, blocks // 2
    for half in range(2):
        part = seats[half * chips : (half + 1) * chips]
        got = jnp.stack([got_ref[seat] for seat in part])
        left_ref[half] = flat(got[:, :rows, :])
        own_ref[half] = got[:, rows:, :].astype(jnp.float32)
    gating_ref[...] = sigmoid(
        jnp.dot(normed_ref[...], gate_ref[...], preferred_element_type=jnp.float32)
    )


def own_part(seats, got, normed, w_gate):
    blocks, both, cols = got.shape
    rows, chips = both // 2, blocks // 2
    return pl.pallas_call(
        functools.partial(own_kernel, seats),
        out_shape=(
            jax.ShapeDtypeStruct((2, chips * rows, cols), jnp.bfloat16),
            jax.ShapeDtypeStruct((2, chips, rows, cols), jnp.float32),
            jax.ShapeDtypeStruct(normed.shape, jnp.float32),
        ),
        in_specs=[VMEM] * 3,
        out_specs=(VMEM,) * 3,
        compiler_params=ROOM,
        cost_estimate=pl.CostEstimate(
            flops=4 * (chips * rows) ** 2 * cols, bytes_accessed=3 * 1024 * 1024, transcendentals=0
        ),
    )(got, normed, w_gate)


def plane_kernel(seats, other_ref, left_ref, own_ref, out_ref):
    blocks, rows, cols = other_ref.shape
    chips = blocks // 2
    plane = jnp.zeros((chips * rows, 2 * chips * rows), jnp.float32)
    first = lax.axis_index("wide") % 2 == 0
    for half in range(2):
        part = seats[half * chips : (half + 1) * chips]
        own = own_ref[half]
        other = jnp.stack([other_ref[seat] for seat in part]).astype(jnp.float32)
        right = jnp.concatenate(
            [jnp.where(first, own, other), jnp.where(first, other, own)], axis=1
        )
        plane += dot_rows(left_ref[half], right.reshape(-1, cols).astype(jnp.bfloat16))
    for half in range(2):
        placed = plane[:, half * cols : (half + 1) * cols].reshape(chips, rows, cols)
        tiles = jnp.concatenate([placed[:, :, : cols // 2], placed[:, :, cols // 2 :]], axis=1)
        tiles = tiles.astype(jnp.bfloat16)
        for chip in range(chips):
            out_ref[seats[half * chips + chip]] = tiles[chip]


def plane_blocks(seats, other, left, own):
    blocks, rows, cols = other.shape
    return pl.pallas_call(
        functools.partial(plane_kernel, seats),
        out_shape=jax.ShapeDtypeStruct((blocks, 2 * rows, cols // 2), jnp.bfloat16),
        in_specs=[VMEM] * 3,
        out_specs=VMEM,
        compiler_params=ROOM,
    )(other, left, own)


def finish_kernel(returned_ref, gating_ref, out_ref, update_hbm, staged, left_device):
    rows, cols, width = staged.shape
    hidden = returned_ref.shape[0]
    turned = jnp.transpose(returned_ref[...], (1, 0, 2))
    copies = []
    for row in range(rows):
        values = jnp.concatenate([turned[row], turned[rows + row]], axis=1).astype(jnp.float32)
        mean = jnp.sum(values, axis=0, keepdims=True) * (1.0 / hidden)
        centered = values - mean
        spread = jnp.sum(centered * centered, axis=0, keepdims=True) * (1.0 / hidden)
        tri_norm = (centered * lax.rsqrt(spread + 1e-05)).astype(jnp.bfloat16)
        mixed = lax.dot_general(
            tri_norm, out_ref[...], (((0,), (0,)), ((), ())), preferred_element_type=jnp.float32
        )
        staged[row] = (gating_ref[pl.ds(row * cols, cols), :] * mixed).astype(jnp.bfloat16)
        copy = pltpu.make_async_copy(staged.at[row], update_hbm.at[row], left_device.at[row])
        copy.start()
        copies.append(copy)
    for copy in copies:
        copy.wait()


def finish(returned, gating, w_out, shape):
    return pl.pallas_call(
        finish_kernel,
        out_shape=jax.ShapeDtypeStruct(shape, jnp.bfloat16),
        in_specs=[VMEM] * 3,
        out_specs=ANY,
        scratch_shapes=[
            pltpu.VMEM(shape, jnp.bfloat16),
            pltpu.SemaphoreType.DMA((shape[0],)),
        ],
        compiler_params=ROOM,
    )(returned, gating, w_out)


def make(wide, row):
    order = group_order(wide // 2, row)
    groups = chip_groups(order, row)
    seats = [order.index(number) for number in range(len(order))]

    def shards(pair, token_valid, w_pair, w_gate, w_out):
        rows = pair.shape[0]
        share, turned, valid, w_gate, w_out = prepare_weights(
            w_pair, token_valid.reshape(1, -1), w_gate, w_out
        )
        normed = norm_pair(pair, share)
        sent = project_blocks(normed, valid, turned, rows, w_out.shape[0])
        got = exchange(sent, groups)
        other = lax.ppermute(got[:, rows:, :], "wide", [(i, i ^ 1) for i in range(wide)])
        left, own, gating = own_part(seats, got, normed, w_gate)
        returned = exchange(plane_blocks(seats, other, left, own), groups)
        return finish(returned, gating, w_out, pair.shape)

    return shards


def solution(mesh):
    placed = (P("wide", "row", None), P(), P(), P(), P())
    return jax.shard_map(
        make(mesh.shape["wide"], mesh.shape["row"]),
        mesh=mesh,
        in_specs=placed,
        out_specs=P("wide", "row", None),
        check_vma=False,
    )
```

```python
import functools

import jax
import jax.numpy as jnp
from jax import lax
from jax.experimental import pallas as pl
from jax.experimental.pallas import tpu as pltpu
from jax.sharding import PartitionSpec as P

VMEM = pl.BlockSpec(memory_space=pltpu.VMEM)
ANY = pl.BlockSpec(memory_space=pl.ANY)
HBM = pl.BlockSpec(memory_space=pltpu.HBM)
ROOM = pltpu.CompilerParams(vmem_limit_bytes=32 * 1024 * 1024)


Y, Z, X = 4, 8, 4
LEAD = (2, 5, 2)


def group_order(chips, row):
    def place(number):
        half, chip = divmod(number, chips)
        x_in = X // row
        return chip // (x_in * Z), chip // x_in % Z, half * x_in + chip % x_in

    def apart(number):
        y, z, x = place(number)
        along = abs(z - LEAD[1])
        return abs(y - LEAD[0]) + min(along, Z - along) + abs(x - LEAD[2])

    return sorted(range(row * chips), key=lambda number: (apart(number) > 0, -apart(number)))


def chip_groups(order, row):
    chips = len(order) // row
    return [
        [(number % chips * 2 + core) * row + number // chips for number in order]
        for core in range(2)
    ]


def exchange(blocks, groups):
    return lax.all_to_all(
        blocks, ("wide", "row"), split_axis=0, concat_axis=0, tiled=True, axis_index_groups=groups
    )


def dot_rows(left, right):
    return lax.dot_general(
        left, right, (((1,), (1,)), ((), ())), preferred_element_type=jnp.float32
    )


def sigmoid(values):
    return 1.0 / (1.0 + jnp.exp(-values))


def weights_kernel(
    w_hbm, valid_hbm, gate_hbm, out_hbm,
    share_ref, turned_ref, valid_ref, gate_ref, out_ref, w_ref, arrived,
):
    part = w_ref.shape[0] // 4
    pieces = [
        (w_hbm.at[pl.ds(at * part, part)], w_ref.at[pl.ds(at * part, part)]) for at in range(4)
    ]
    pieces += [(valid_hbm, valid_ref), (gate_hbm, gate_ref), (out_hbm, out_ref)]
    copies = [
        pltpu.make_async_copy(source, target, arrived.at[index])
        for index, (source, target) in enumerate(pieces)
    ]
    for copy in copies:
        copy.start()
    share_ref[...] = jnp.full(share_ref.shape, 1.0 / share_ref.shape[1], jnp.bfloat16)
    for copy in copies[:4]:
        copy.wait()
    turned_ref[...] = w_ref[...].T
    for copy in copies[4:]:
        copy.wait()


def prepare_weights(w_pair, valid, w_gate, w_out):
    width, outs = w_pair.shape
    return pl.pallas_call(
        weights_kernel,
        out_shape=(
            jax.ShapeDtypeStruct((2 * width, width), jnp.bfloat16),
            jax.ShapeDtypeStruct((outs, width), jnp.bfloat16),
            jax.ShapeDtypeStruct(valid.shape, jnp.int32),
            jax.ShapeDtypeStruct(w_gate.shape, jnp.bfloat16),
            jax.ShapeDtypeStruct(w_out.shape, jnp.bfloat16),
        ),
        in_specs=[HBM] * 4,
        out_specs=(VMEM,) * 5,
        scratch_shapes=[
            pltpu.VMEM(w_pair.shape, jnp.bfloat16),
            pltpu.SemaphoreType.DMA((7,)),
        ],
        compiler_params=ROOM,
        cost_estimate=pl.CostEstimate(
            flops=1024**3, bytes_accessed=8 * 1024 * 1024, transcendentals=0
        ),
    )(
        *(
            pltpu.with_memory_space_constraint(value, pltpu.HBM)
            for value in (w_pair, valid, w_gate, w_out)
        )
    )


def normed_kernel(pair_ref, share_ref, normed_ref):
    rows, cols, width = pair_ref.shape

    def mean(values):
        return jnp.dot(
            values, share_ref[: values.shape[1], :], preferred_element_type=jnp.float32
        )

    step = rows // 2
    for first in range(0, rows, step):
        values = pair_ref[pl.ds(first, step)].reshape(step * cols, width)
        centered = values.astype(jnp.float32) - mean(values)
        square = centered * centered
        high = square.astype(jnp.bfloat16)
        low = (square - high.astype(jnp.float32)).astype(jnp.bfloat16)
        spread = mean(jnp.concatenate([high, low], axis=1))
        normed_ref[pl.ds(first * cols, step * cols), :] = (
            centered * lax.rsqrt(spread + 1e-05)
        ).astype(jnp.bfloat16)


def norm_pair(pair, share):
    rows, cols, width = pair.shape
    return pl.pallas_call(
        normed_kernel,
        out_shape=jax.ShapeDtypeStruct((rows * cols, width), jnp.bfloat16),
        in_specs=[VMEM] * 2,
        out_specs=VMEM,
        compiler_params=ROOM,
        cost_estimate=pl.CostEstimate(
            flops=8 * rows * cols * width * width, bytes_accessed=4 * 1024 * 1024, transcendentals=0
        ),
    )(pair, share)


def project_kernel(normed_ref, valid_ref, turned_ref, sent_ref, held):
    hidden, both, cols = sent_ref.shape
    rows = both // 2
    valid = valid_ref[...].astype(jnp.float32)
    seat = lax.broadcasted_iota(jnp.int32, valid.shape, 1)
    first = lax.axis_index("wide") * rows
    col_valid = jnp.where(lax.axis_index("row") == 0, valid[:, :cols], valid[:, cols:])
    for row in range(rows):
        row_valid = jnp.sum(jnp.where(seat == first + row, valid, 0.0), axis=1, keepdims=True)
        mask = row_valid * col_valid
        proj = dot_rows(turned_ref[...], normed_ref[pl.ds(row * cols, cols), :])
        left = sigmoid(proj[:hidden]) * proj[hidden : 2 * hidden] * mask
        right = sigmoid(proj[2 * hidden : 3 * hidden]) * proj[3 * hidden :] * mask
        held[rows + row] = left.astype(jnp.bfloat16)
        held[row] = right.astype(jnp.bfloat16)
    step = 16
    for first_channel in range(0, hidden, step):
        part = slice(first_channel, first_channel + step)
        sent_ref[part] = jnp.transpose(held[:, part, :], (1, 0, 2))


def project_blocks(normed, valid, turned, rows, hidden):
    cols = normed.shape[0] // rows
    return pl.pallas_call(
        project_kernel,
        out_shape=jax.ShapeDtypeStruct((hidden, 2 * rows, cols), jnp.bfloat16),
        in_specs=[VMEM] * 3,
        out_specs=VMEM,
        scratch_shapes=[pltpu.VMEM((2 * rows, hidden, cols), jnp.bfloat16)],
        compiler_params=ROOM,
    )(normed, valid, turned)


def flat(values):
    chips, rows, cols = values.shape
    return values.astype(jnp.float32).reshape(chips * rows, cols).astype(jnp.bfloat16)


def own_kernel(seats, got_ref, normed_ref, gate_ref, left_ref, own_ref, gating_ref):
    blocks, both, cols = got_ref.shape
    rows, chips = both // 2, blocks // 2
    for half in range(2):
        part = seats[half * chips : (half + 1) * chips]
        got = jnp.stack([got_ref[seat] for seat in part])
        left_ref[half] = flat(got[:, rows:, :])
        own_ref[half] = got[:, :rows, :].astype(jnp.float32)
    gating_ref[...] = sigmoid(
        jnp.dot(normed_ref[...], gate_ref[...], preferred_element_type=jnp.float32)
    )


def own_part(seats, got, normed, w_gate):
    blocks, both, cols = got.shape
    rows, chips = both // 2, blocks // 2
    return pl.pallas_call(
        functools.partial(own_kernel, seats),
        out_shape=(
            jax.ShapeDtypeStruct((2, chips * rows, cols), jnp.bfloat16),
            jax.ShapeDtypeStruct((2, chips, rows, cols), jnp.float32),
            jax.ShapeDtypeStruct(normed.shape, jnp.float32),
        ),
        in_specs=[VMEM] * 3,
        out_specs=(VMEM,) * 3,
        compiler_params=ROOM,
        cost_estimate=pl.CostEstimate(
            flops=4 * (chips * rows) ** 2 * cols, bytes_accessed=3 * 1024 * 1024, transcendentals=0
        ),
    )(got, normed, w_gate)


def plane_kernel(seats, other_ref, left_ref, own_ref, out_ref):
    blocks, rows, cols = other_ref.shape
    chips = blocks // 2
    plane = jnp.zeros((chips * rows, 2 * chips * rows), jnp.float32)
    first = lax.axis_index("wide") % 2 == 0
    for half in range(2):
        part = seats[half * chips : (half + 1) * chips]
        own = own_ref[half]
        other = jnp.stack([other_ref[seat] for seat in part]).astype(jnp.float32)
        right = jnp.concatenate(
            [jnp.where(first, own, other), jnp.where(first, other, own)], axis=1
        )
        plane += dot_rows(left_ref[half], right.reshape(-1, cols).astype(jnp.bfloat16))
    for half in range(2):
        placed = plane[:, half * cols : (half + 1) * cols].reshape(chips, rows, cols)
        tiles = jnp.concatenate([placed[:, :, : cols // 2], placed[:, :, cols // 2 :]], axis=1)
        tiles = tiles.astype(jnp.bfloat16)
        for chip in range(chips):
            out_ref[seats[half * chips + chip]] = tiles[chip]


def plane_blocks(seats, other, left, own):
    blocks, rows, cols = other.shape
    return pl.pallas_call(
        functools.partial(plane_kernel, seats),
        out_shape=jax.ShapeDtypeStruct((blocks, 2 * rows, cols // 2), jnp.bfloat16),
        in_specs=[VMEM] * 3,
        out_specs=VMEM,
        compiler_params=ROOM,
    )(other, left, own)


def finish_kernel(returned_ref, gating_ref, out_ref, update_hbm, staged, left_device):
    rows, cols, width = staged.shape
    hidden = returned_ref.shape[0]
    turned = jnp.transpose(returned_ref[...], (1, 0, 2))
    copies = []
    for row in range(rows):
        values = jnp.concatenate([turned[row], turned[rows + row]], axis=1).astype(jnp.float32)
        mean = jnp.sum(values, axis=0, keepdims=True) * (1.0 / hidden)
        centered = values - mean
        spread = jnp.sum(centered * centered, axis=0, keepdims=True) * (1.0 / hidden)
        tri_norm = (centered * lax.rsqrt(spread + 1e-05)).astype(jnp.bfloat16)
        mixed = lax.dot_general(
            tri_norm, out_ref[...], (((0,), (0,)), ((), ())), preferred_element_type=jnp.float32
        )
        staged[row] = (gating_ref[pl.ds(row * cols, cols), :] * mixed).astype(jnp.bfloat16)
        copy = pltpu.make_async_copy(staged.at[row], update_hbm.at[row], left_device.at[row])
        copy.start()
        copies.append(copy)
    for copy in copies:
        copy.wait()


def finish(returned, gating, w_out, shape):
    return pl.pallas_call(
        finish_kernel,
        out_shape=jax.ShapeDtypeStruct(shape, jnp.bfloat16),
        in_specs=[VMEM] * 3,
        out_specs=ANY,
        scratch_shapes=[
            pltpu.VMEM(shape, jnp.bfloat16),
            pltpu.SemaphoreType.DMA((shape[0],)),
        ],
        compiler_params=ROOM,
    )(returned, gating, w_out)


def make(wide, row):
    order = group_order(wide // 2, row)
    groups = chip_groups(order, row)
    seats = [order.index(number) for number in range(len(order))]

    def shards(pair, token_valid, w_pair, w_gate, w_out):
        rows = pair.shape[0]
        share, turned, valid, w_gate, w_out = prepare_weights(
            w_pair, token_valid.reshape(1, -1), w_gate, w_out
        )
        normed = norm_pair(pair, share)
        sent = project_blocks(normed, valid, turned, rows, w_out.shape[0])
        got = exchange(sent, groups)
        other = lax.ppermute(got[:, :rows, :], "wide", [(i, i ^ 1) for i in range(wide)])
        left, own, gating = own_part(seats, got, normed, w_gate)
        returned = exchange(plane_blocks(seats, other, left, own), groups)
        return finish(returned, gating, w_out, pair.shape)

    return shards


def solution(mesh):
    placed = (P("wide", "row", None), P(), P(), P(), P())
    return jax.shard_map(
        make(mesh.shape["wide"], mesh.shape["row"]),
        mesh=mesh,
        in_specs=placed,
        out_specs=P("wide", "row", None),
        check_vma=False,
    )
```

```python
import functools

import jax
import jax.numpy as jnp
from jax import lax
from jax.experimental import pallas as pl
from jax.experimental.pallas import tpu as pltpu
from jax.sharding import PartitionSpec as P

VMEM = pl.BlockSpec(memory_space=pltpu.VMEM)
ANY = pl.BlockSpec(memory_space=pl.ANY)
HBM = pl.BlockSpec(memory_space=pltpu.HBM)
ROOM = pltpu.CompilerParams(vmem_limit_bytes=32 * 1024 * 1024)


Y, Z, X = 4, 8, 4
LEAD = (2, 5, 2)


def group_order(chips, row):
    def place(number):
        half, chip = divmod(number, chips)
        x_in = X // row
        return chip // (x_in * Z), chip // x_in % Z, half * x_in + chip % x_in

    def apart(number):
        y, z, x = place(number)
        along = abs(z - LEAD[1])
        return abs(y - LEAD[0]) + min(along, Z - along) + abs(x - LEAD[2])

    return sorted(range(row * chips), key=lambda number: (apart(number) > 0, -apart(number)))


def chip_groups(order, row):
    chips = len(order) // row
    return [
        [(number % chips * 2 + core) * row + number // chips for number in order]
        for core in range(2)
    ]


def exchange(blocks, groups):
    return lax.all_to_all(
        blocks, ("wide", "row"), split_axis=0, concat_axis=0, tiled=True, axis_index_groups=groups
    )


def dot_rows(left, right):
    return lax.dot_general(
        left, right, (((1,), (1,)), ((), ())), preferred_element_type=jnp.float32
    )


def sigmoid(values):
    return 1.0 / (1.0 + jnp.exp(-values))


def weights_kernel(w_hbm, valid_hbm, share_ref, turned_ref, valid_ref, w_ref, arrived):
    part = w_ref.shape[0] // 4
    pieces = [
        (w_hbm.at[pl.ds(at * part, part)], w_ref.at[pl.ds(at * part, part)]) for at in range(4)
    ]
    pieces += [(valid_hbm, valid_ref)]
    copies = [
        pltpu.make_async_copy(source, target, arrived.at[index])
        for index, (source, target) in enumerate(pieces)
    ]
    for copy in copies:
        copy.start()
    share_ref[...] = jnp.full(share_ref.shape, 1.0 / share_ref.shape[1], jnp.bfloat16)
    for copy in copies:
        copy.wait()
    turned_ref[...] = w_ref[...].T


def prepare_weights(w_pair, valid):
    width, outs = w_pair.shape
    return pl.pallas_call(
        weights_kernel,
        out_shape=(
            jax.ShapeDtypeStruct((2 * width, width), jnp.bfloat16),
            jax.ShapeDtypeStruct((outs, width), jnp.bfloat16),
            jax.ShapeDtypeStruct(valid.shape, jnp.int32),
        ),
        in_specs=[HBM] * 2,
        out_specs=(VMEM,) * 3,
        scratch_shapes=[
            pltpu.VMEM(w_pair.shape, jnp.bfloat16),
            pltpu.SemaphoreType.DMA((5,)),
        ],
        compiler_params=ROOM,
        cost_estimate=pl.CostEstimate(
            flops=1024**3, bytes_accessed=8 * 1024 * 1024, transcendentals=0
        ),
    )(*(pltpu.with_memory_space_constraint(value, pltpu.HBM) for value in (w_pair, valid)))


def normed_kernel(pair_ref, share_ref, normed_ref):
    rows, cols, width = pair_ref.shape

    def mean(values):
        return jnp.dot(
            values, share_ref[: values.shape[1], :], preferred_element_type=jnp.float32
        )

    step = rows // 2
    for first in range(0, rows, step):
        values = pair_ref[pl.ds(first, step)].reshape(step * cols, width)
        centered = values.astype(jnp.float32) - mean(values)
        square = centered * centered
        high = square.astype(jnp.bfloat16)
        low = (square - high.astype(jnp.float32)).astype(jnp.bfloat16)
        spread = mean(jnp.concatenate([high, low], axis=1))
        normed_ref[pl.ds(first * cols, step * cols), :] = (
            centered * lax.rsqrt(spread + 1e-05)
        ).astype(jnp.bfloat16)


def norm_pair(pair, share):
    rows, cols, width = pair.shape
    return pl.pallas_call(
        normed_kernel,
        out_shape=jax.ShapeDtypeStruct((rows * cols, width), jnp.bfloat16),
        in_specs=[VMEM] * 2,
        out_specs=VMEM,
        compiler_params=ROOM,
        cost_estimate=pl.CostEstimate(
            flops=8 * rows * cols * width * width, bytes_accessed=4 * 1024 * 1024, transcendentals=0
        ),
    )(pair, share)


def project_kernel(normed_ref, valid_ref, turned_ref, sent_ref, held):
    hidden, both, cols = sent_ref.shape
    rows = both // 2
    valid = valid_ref[...].astype(jnp.float32)
    seat = lax.broadcasted_iota(jnp.int32, valid.shape, 1)
    first = lax.axis_index("wide") * rows
    col_valid = jnp.where(lax.axis_index("row") == 0, valid[:, :cols], valid[:, cols:])
    for side in range(2):
        gate_rows = pl.ds(2 * side * hidden, hidden)
        value_rows = pl.ds((2 * side + 1) * hidden, hidden)
        for row in range(rows):
            row_valid = jnp.sum(jnp.where(seat == first + row, valid, 0.0), axis=1, keepdims=True)
            normed = normed_ref[pl.ds(row * cols, cols), :]
            gate = sigmoid(dot_rows(turned_ref[gate_rows, :], normed))
            value = dot_rows(turned_ref[value_rows, :], normed)
            mask = row_valid * col_valid
            held[side * rows + row] = (gate * value * mask).astype(jnp.bfloat16)
    step = 16
    for first_channel in range(0, hidden, step):
        part = slice(first_channel, first_channel + step)
        sent_ref[part] = jnp.transpose(held[:, part, :], (1, 0, 2))


def project_blocks(normed, valid, turned, rows, hidden):
    cols = normed.shape[0] // rows
    return pl.pallas_call(
        project_kernel,
        out_shape=jax.ShapeDtypeStruct((hidden, 2 * rows, cols), jnp.bfloat16),
        in_specs=[VMEM] * 3,
        out_specs=VMEM,
        scratch_shapes=[pltpu.VMEM((2 * rows, hidden, cols), jnp.bfloat16)],
        compiler_params=ROOM,
    )(normed, valid, turned)


def flat(values):
    chips, rows, cols = values.shape
    return values.astype(jnp.float32).reshape(chips * rows, cols).astype(jnp.bfloat16)


def own_kernel(
    seats, got_ref, normed_ref, gate_ref, w_out_ref, left_ref, own_ref, gating_ref, held_out_ref
):
    held_out_ref[...] = w_out_ref[...]
    blocks, both, cols = got_ref.shape
    rows, chips = both // 2, blocks // 2
    for half in range(2):
        part = seats[half * chips : (half + 1) * chips]
        got = jnp.stack([got_ref[seat] for seat in part])
        left_ref[half] = flat(got[:, :rows, :])
        own_ref[half] = got[:, rows:, :].astype(jnp.float32)
    gating_ref[...] = sigmoid(
        jnp.dot(normed_ref[...], gate_ref[...], preferred_element_type=jnp.float32)
    )


def own_part(seats, got, normed, w_gate, w_out):
    blocks, both, cols = got.shape
    rows, chips = both // 2, blocks // 2
    return pl.pallas_call(
        functools.partial(own_kernel, seats),
        out_shape=(
            jax.ShapeDtypeStruct((2, chips * rows, cols), jnp.bfloat16),
            jax.ShapeDtypeStruct((2, chips, rows, cols), jnp.float32),
            jax.ShapeDtypeStruct(normed.shape, jnp.float32),
            jax.ShapeDtypeStruct(w_out.shape, jnp.bfloat16),
        ),
        in_specs=[VMEM] * 4,
        out_specs=(VMEM,) * 4,
        compiler_params=ROOM,
        cost_estimate=pl.CostEstimate(
            flops=4 * (chips * rows) ** 2 * cols, bytes_accessed=3 * 1024 * 1024, transcendentals=0
        ),
    )(got, normed, w_gate, w_out)


def plane_kernel(seats, other_ref, left_ref, own_ref, out_ref):
    blocks, rows, cols = other_ref.shape
    chips = blocks // 2
    plane = jnp.zeros((chips * rows, 2 * chips * rows), jnp.float32)
    first = lax.axis_index("wide") % 2 == 0
    for half in range(2):
        part = seats[half * chips : (half + 1) * chips]
        own = own_ref[half]
        other = jnp.stack([other_ref[seat] for seat in part]).astype(jnp.float32)
        right = jnp.concatenate(
            [jnp.where(first, own, other), jnp.where(first, other, own)], axis=1
        )
        plane += dot_rows(left_ref[half], right.reshape(-1, cols).astype(jnp.bfloat16))
    for half in range(2):
        placed = plane[:, half * cols : (half + 1) * cols].reshape(chips, rows, cols)
        tiles = jnp.concatenate([placed[:, :, : cols // 2], placed[:, :, cols // 2 :]], axis=1)
        tiles = tiles.astype(jnp.bfloat16)
        for chip in range(chips):
            out_ref[seats[half * chips + chip]] = tiles[chip]


def plane_blocks(seats, other, left, own):
    blocks, rows, cols = other.shape
    return pl.pallas_call(
        functools.partial(plane_kernel, seats),
        out_shape=jax.ShapeDtypeStruct((blocks, 2 * rows, cols // 2), jnp.bfloat16),
        in_specs=[VMEM] * 3,
        out_specs=VMEM,
        compiler_params=ROOM,
    )(other, left, own)


def finish_kernel(returned_ref, gating_ref, out_ref, update_hbm, staged, left_device):
    rows, cols, width = staged.shape
    hidden = returned_ref.shape[0]
    turned = jnp.transpose(returned_ref[...], (1, 0, 2))
    copies = []
    for row in range(rows):
        values = jnp.concatenate([turned[row], turned[rows + row]], axis=1).astype(jnp.float32)
        mean = jnp.sum(values, axis=0, keepdims=True) * (1.0 / hidden)
        centered = values - mean
        spread = jnp.sum(centered * centered, axis=0, keepdims=True) * (1.0 / hidden)
        tri_norm = (centered * lax.rsqrt(spread + 1e-05)).astype(jnp.bfloat16)
        mixed = lax.dot_general(
            tri_norm, out_ref[...], (((0,), (0,)), ((), ())), preferred_element_type=jnp.float32
        )
        staged[row] = (gating_ref[pl.ds(row * cols, cols), :] * mixed).astype(jnp.bfloat16)
        copy = pltpu.make_async_copy(staged.at[row], update_hbm.at[row], left_device.at[row])
        copy.start()
        copies.append(copy)
    for copy in copies:
        copy.wait()


def finish(returned, gating, w_out, shape):
    return pl.pallas_call(
        finish_kernel,
        out_shape=jax.ShapeDtypeStruct(shape, jnp.bfloat16),
        in_specs=[VMEM] * 3,
        out_specs=ANY,
        scratch_shapes=[
            pltpu.VMEM(shape, jnp.bfloat16),
            pltpu.SemaphoreType.DMA((shape[0],)),
        ],
        compiler_params=ROOM,
    )(returned, gating, w_out)


def make(wide, row):
    order = group_order(wide // 2, row)
    groups = chip_groups(order, row)
    seats = [order.index(number) for number in range(len(order))]

    def shards(pair, token_valid, w_pair, w_gate, w_out):
        rows = pair.shape[0]
        share, turned, valid = prepare_weights(w_pair, token_valid.reshape(1, -1))
        normed = norm_pair(pair, share)
        sent = project_blocks(normed, valid, turned, rows, w_out.shape[0])
        got = exchange(sent, groups)
        other = lax.ppermute(got[:, rows:, :], "wide", [(i, i ^ 1) for i in range(wide)])
        left, own, gating, w_out = own_part(seats, got, normed, w_gate, w_out)
        returned = exchange(plane_blocks(seats, other, left, own), groups)
        return finish(returned, gating, w_out, pair.shape)

    return shards


def solution(mesh):
    placed = (P("wide", "row", None), P(), P(), P(), P())
    return jax.shard_map(
        make(mesh.shape["wide"], mesh.shape["row"]),
        mesh=mesh,
        in_specs=placed,
        out_specs=P("wide", "row", None),
        check_vma=False,
    )
```
